32 devices in a mesh: seq: 16 (over z, y, x), head: 2 (over core).
Axes of the slice: x: 2, y: 2, z: 4, core: 2. Of those that a mesh axis runs over, the one named last changes fastest.
Arguments:
- values: bfloat16 [2, 1024, 4096], P(None, 'seq', 'head'), may hold values from -6 to 6
- keys_b: bfloat16 [2, 1024, 128], P(None, 'seq'), may hold values from -0.29882812 to 0.29882812
- queries_c: bfloat16 [2, 1024, 128], P(None, 'seq'), may hold values from -0.29882812 to 0.29882812
- forget: float32 [2, 64, 1024], P(None, 'head', 'seq'), may hold values from 0 to 2
- skip: float32 [64], P('head'), may hold values from 0.5 to 1.5
- cotangent: bfloat16 [2, 1024, 4096], P(None, 'seq', 'head'), may hold values from -0.59765625 to 0.59765625
Outputs:
- mixed: bfloat16 [2, 1024, 4096], P(None, 'seq', 'head')
- grad_values: bfloat16 [2, 1024, 4096], P(None, 'seq', 'head')
- grad_bc: float32 [2, 2, 1024, 128], P(None, None, ('seq', 'head'))
The draws below stay inside these ranges and needn't reach their ends.
All inputs are finite; a program needn't handle non-finite values.
Results may differ from the reference program's by a relative error of at most 0.012.
Values sent between devices are 32-bit elements; how exact they have to be, the bound alone decides.
No kernel may reach another device: no remote copies, remote signals or barrier semaphores. Data moves between devices by JAX's collectives and lax.ppermute only.
A program may use at most 128 MiB of HBM per device.

```python
import math
import jax
import jax.numpy as jnp
from jax import lax

HEADS = 64
HEAD_DIM = 64
STATE = 128
SEQS = 2
SEQ_DEV = 64
WIDTH = 4096
LENGTH = 1024


def draw_forget(key, part):
    streams = jax.random.split(key, 6)
    blocks = LENGTH // SEQ_DEV
    slow_share = 0.5
    slow = jax.random.uniform(streams[0], (SEQS, HEADS, 1)) < slow_share
    fast_rate = jnp.exp(jax.random.uniform(streams[1], (SEQS, HEADS, 1), minval=math.log(1.0 / 50.0), maxval=math.log(1.0 / 30.0)))
    forgetting_speed = jnp.where(slow, 0.6 / LENGTH, fast_rate)
    approximate_guess = jnp.exp(jax.random.uniform(streams[2], (SEQS, HEADS, LENGTH), minval=math.log(0.5), maxval=math.log(2.0)))
    processor_factor = jnp.exp(jax.random.uniform(streams[3], (SEQS, 1, blocks, 1), minval=math.log(0.7), maxval=math.log(1.4)))
    processor_factor = jnp.broadcast_to(processor_factor, (SEQS, 1, blocks, SEQ_DEV)).reshape(SEQS, 1, LENGTH)
    probe_locations = jax.random.randint(streams[4], (SEQS, 1, 1, 2), 0, LENGTH)
    recurrence_levels = jax.random.uniform(streams[5], (SEQS, 1, 1, 2), minval=0.25, maxval=0.7)
    token_offset = jnp.arange(LENGTH)[None, None, :, None]
    span_count = jnp.sum(jnp.where(token_offset == probe_locations, recurrence_levels, 0.0), axis=-1)
    return (forgetting_speed * approximate_guess * processor_factor + span_count).astype(jnp.float32)


def levels(stream_key, shape, cuts, least, largest):
    loudness, own = 1.0, jax.random.fold_in(stream_key, 6)
    for dim, blocks in cuts:
        steps = jnp.exp(jax.random.uniform(jax.random.fold_in(own, dim), (blocks,), jnp.float32, least / len(cuts), largest / len(cuts)))
        loudness = loudness * jnp.repeat(steps, shape[dim] // blocks).reshape([-1 if axis == dim else 1 for axis in range(len(shape))])
    return loudness


def gaussian(rng, shape, scale, limit, cuts=(), kind=jnp.bfloat16):
    drawn = jax.random.normal(rng, shape, jnp.float32) * scale
    if len(cuts) > 0:
        drawn = levels(rng, shape, cuts, -0.22, 0.18) * drawn
    return jnp.clip(drawn, min=-limit, max=limit).astype(kind)


def setup_inputs(seed: int = 0) -> dict:
    splits = jax.random.split(jax.random.key(seed), 7)
    return {
        "values": gaussian(splits[0], (SEQS, LENGTH, WIDTH), 1.0, 6.0, ((1, 16), (2, 2))),
        "keys_b": gaussian(splits[1], (SEQS, LENGTH, STATE), 0.05, 0.29882812, ((1, 16),)),
        "queries_c": gaussian(splits[2], (SEQS, LENGTH, STATE), 0.05, 0.29882812, ((1, 16),)),
        "forget": draw_forget(jax.random.fold_in(splits[6], 71), 0),
        "skip": jnp.clip(0.5 + 1.0 * jax.random.uniform(splits[4], (HEADS,), jnp.float32) ** levels(splits[4], (HEADS,), ((0, 2),), -0.2, 0.2), 0.5, 1.5),
        "cotangent": gaussian(splits[5], (SEQS, LENGTH, WIDTH), 0.1, 0.59765625, ((1, 16), (2, 2))),
    }


def own_state(values, keys_wide, logcum):
    seq_count, rows, wide = values.shape
    head_count = logcum.shape[1]
    tail_decay = jnp.exp(logcum[..., -1:] - logcum)
    scaled = values.astype(jnp.float32).reshape(seq_count, rows, head_count, wide // head_count)
    scaled = scaled * jnp.transpose(tail_decay, (0, 2, 1))[..., None]
    return jnp.einsum('suhp,sun->shpn', scaled, keys_wide, precision=lax.Precision.HIGHEST)

def read_state(queries_wide, logcum, carried):
    inner_part = jnp.einsum('stn,shpn->sthp', queries_wide, carried, precision=lax.Precision.HIGHEST)
    return inner_part * jnp.transpose(jnp.exp(logcum), (0, 2, 1))[..., None]

def block_scores(queries_c, keys_b):
    return jnp.einsum('stn,sun->stu', queries_c, keys_b, preferred_element_type=jnp.float32)

def block_pass(values, keys_wide, queries_wide, scores, forget, skip, carried):
    seq_count, rows, wide = values.shape
    head_count = skip.shape[0]
    head_width = wide // head_count
    logcum = jnp.cumsum(-forget, axis=-1)
    causal = jnp.arange(rows)[:, None] >= jnp.arange(rows)[None, :]
    log_gap = logcum[..., :, None] - logcum[..., None, :]
    decay_mask = jnp.where(causal, jnp.exp(jnp.where(causal, log_gap, 0.0)), 0.0)
    weights = (scores[:, None] * decay_mask).astype(jnp.bfloat16)
    by_head = values.reshape(seq_count, rows, head_count, head_width)
    own_part = jnp.einsum('shtu,suhp->sthp', weights, by_head, preferred_element_type=jnp.float32)
    summed = own_part + read_state(queries_wide, logcum, carried) + skip[:, None] * by_head.astype(jnp.float32)
    mixed = summed.reshape(seq_count, rows, wide).astype(jnp.bfloat16)
    final_state = jnp.exp(logcum[..., -1])[..., None, None] * carried + own_state(values, keys_wide, logcum)
    return (mixed, final_state)

def reference(values, keys_b, queries_c, forget, skip, cotangent):
    blocks = LENGTH // SEQ_DEV

    def to_blocks(array):
        return jnp.transpose(array.reshape(SEQS, blocks, SEQ_DEV, array.shape[-1]), (1, 0, 2, 3))

    def from_blocks(array):
        return jnp.transpose(array, (1, 0, 2, 3)).reshape(SEQS, LENGTH, array.shape[-1])
    forget_blocks = jnp.transpose(forget.reshape(SEQS, HEADS, blocks, SEQ_DEV), (2, 0, 1, 3))
    key_blocks = to_blocks(keys_b)
    query_blocks = to_blocks(queries_c)
    score_blocks = lax.map(lambda pair: block_scores(pair[0], pair[1]), (query_blocks, key_blocks))
    key_wide = key_blocks.astype(jnp.float32)
    query_wide = query_blocks.astype(jnp.float32)

    def forward(value_blocks, key_all, query_all, score_all, forget_all):

        def block_step(carried, pieces):
            mixed, final_state = block_pass(pieces[0], pieces[1], pieces[2], pieces[3], pieces[4], skip, carried)
            return (final_state, mixed)
        start = jnp.zeros((SEQS, HEADS, HEAD_DIM, STATE), jnp.float32)
        _, outputs = lax.scan(jax.checkpoint(block_step), start, (value_blocks, key_all, query_all, score_all, forget_all))
        return outputs
    outputs, pullback = jax.vjp(forward, to_blocks(values), key_wide, query_wide, score_blocks, forget_blocks)
    grads = pullback(to_blocks(cotangent))
    score_grad = grads[3]
    grad_query = grads[2] + jnp.einsum('bstu,bsun->bstn', score_grad, key_wide, precision=lax.Precision.HIGHEST)
    grad_key = grads[1] + jnp.einsum('bstu,bstn->bsun', score_grad, query_wide, precision=lax.Precision.HIGHEST)
    mixed = from_blocks(outputs)
    grad_values = from_blocks(grads[0])
    grad_bc = jnp.stack([from_blocks(grad_key), from_blocks(grad_query)])
    return (mixed, grad_values, grad_bc)
```

```python
import functools

import jax
import jax.numpy as jnp
from jax import lax
from jax.experimental import pallas as pl
from jax.experimental.pallas import tpu as pltpu
from jax.sharding import PartitionSpec as P

F32, BF16 = jnp.float32, jnp.bfloat16
LANES = 128
VMEM = pltpu.CompilerParams(vmem_limit_bytes=48 * 1024 * 1024)


def nn(a, b):
    return lax.dot_general(a, b, (((1,), (0,)), ((), ())), preferred_element_type=F32)


def nt(a, b):
    return lax.dot_general(a, b, (((1,), (1,)), ((), ())), preferred_element_type=F32)


def tn(a, b):
    return lax.dot_general(a, b, (((0,), (0,)), ((), ())), preferred_element_type=F32)


def rows_of(block, rows):
    return pl.ds(pl.multiple_of(block * rows, rows), rows)


def pack_kernel(dims, where, values, cotangent, keys, queries, forget, *pieces):
    g, rows, tiles, heads = dims
    mine = where[0]
    upto = lax.broadcasted_iota(jnp.int32, (rows, rows), 0) <= lax.broadcasted_iota(
        jnp.int32, (rows, rows), 1
    )
    logcum = -lax.dot_general(
        forget[...],
        upto.astype(F32),
        (((1,), (0,)), ((), ())),
        precision=lax.Precision.HIGHEST,
        preferred_element_type=F32,
    )
    held = jnp.concatenate([logcum, jnp.zeros_like(logcum)], axis=1)
    keys_wide = keys[...].astype(F32)
    queries_wide = queries[...].astype(F32)
    for d in range(g):
        to = lax.bitwise_xor(mine, d)
        piece = pieces[d]
        for k in range(tiles):
            lanes = pl.ds(pl.multiple_of((to * tiles + k) * LANES, LANES), LANES)
            piece[k * rows : (k + 1) * rows, :] = values[:, lanes].astype(F32)
            piece[(tiles + k) * rows : (tiles + k + 1) * rows, :] = cotangent[:, lanes].astype(F32)
        piece[2 * tiles * rows : (2 * tiles + 1) * rows, :] = keys_wide
        piece[(2 * tiles + 1) * rows : (2 * tiles + 2) * rows, :] = queries_wide
        part = jnp.zeros((heads, LANES), F32)
        for j in range(g):
            part = jnp.where(to == j, held[j * heads : (j + 1) * heads], part)
        piece[(2 * tiles + 2) * rows : (2 * tiles + 2) * rows + heads, :] = part
        piece[(2 * tiles + 2) * rows + heads :, :] = jnp.zeros((8 - heads, LANES), F32)


def spread(columns, heads, tiles):
    per = heads // tiles
    width = LANES // per
    lane = lax.broadcasted_iota(jnp.int32, (columns.shape[0], LANES), 1)
    out = []
    for k in range(tiles):
        wide = jnp.broadcast_to(columns[:, k * per : k * per + 1], lane.shape)
        for e in range(1, per):
            h = k * per + e
            wide = jnp.where(lane >= e * width, columns[:, h : h + 1], wide)
        out.append(wide)
    return jnp.concatenate(out, axis=1) if tiles > 1 else out[0]


def local_kernel(dims, where, skip, *refs):
    g, rows, tiles, heads = dims
    pieces, refs = refs[:g], refs[g:]
    (mixed, grad_v, grad_c, grad_b, v_tail, dy_head, keys, queries, cols, ahead, behind, decay) = refs[:12]
    v_all, dy_all, log_blocks = refs[12:]
    window = g * rows
    width = tiles * LANES
    head_width = width // heads
    mine = where[0]
    for d in range(g):
        piece = pieces[d]
        at = lax.bitwise_xor(mine, d)
        here = rows_of(at, rows)
        for k in range(tiles):
            lanes = slice(k * LANES, (k + 1) * LANES)
            v_all[here, lanes] = piece[k * rows : (k + 1) * rows, :].astype(BF16)
            dy_all[here, lanes] = piece[(tiles + k) * rows : (tiles + k + 1) * rows, :].astype(BF16)
        keys[here, :] = piece[2 * tiles * rows : (2 * tiles + 1) * rows, :].astype(BF16)
        queries[here, :] = piece[(2 * tiles + 1) * rows : (2 * tiles + 2) * rows, :].astype(BF16)
        log_blocks[at] = piece[(2 * tiles + 2) * rows :, :]
    before = jnp.zeros((8, 1), F32)
    parts = []
    for j in range(g):
        block = log_blocks[j][:, :rows] + before
        before = block[:, rows - 1 : rows]
        parts.append(block)
    log_rows = jnp.concatenate(parts, axis=1)
    log_cols = jnp.transpose(log_rows)[:, :heads]
    last = before
    head_decay = spread(jnp.exp(log_cols), heads, tiles)
    tail_decay = spread(jnp.exp(log_cols[window - 1 : window, :] - log_cols), heads, tiles)
    cols[...] = jnp.zeros_like(cols)
    cols[:, :heads] = log_cols
    decay[...] = jnp.broadcast_to(head_decay[window - 1 : window, :], decay.shape)
    v = v_all[...]
    dy = dy_all[...]
    v_wide = v.astype(F32)
    dy_wide = dy.astype(F32)
    v_tail[...] = (v_wide * tail_decay).astype(BF16)
    dy_head[...] = (dy_wide * head_decay).astype(BF16)
    ahead[...] = tn(keys[...], v_tail[...])
    behind[...] = tn(queries[...], dy_head[...])
    mixed[...] = v_wide * skip[...]
    dy_t = jnp.transpose(dy)
    tile = min(window, 256)
    causal = lax.broadcasted_iota(jnp.int32, (tile, tile), 0) >= lax.broadcasted_iota(
        jnp.int32, (tile, tile), 1
    )
    count = window // tile
    dv_t = [[None] * count for _ in range(heads)]
    for q in range(count):
        t = slice(q * tile, (q + 1) * tile)
        for r in range(q + 1):
            u = slice(r * tile, (r + 1) * tile)
            scores = nt(queries[t, :], keys[u, :])
            score_grad = jnp.zeros((tile, tile), F32)
            for h in range(heads):
                lanes = slice(h * head_width, (h + 1) * head_width)
                gap = log_cols[t, h : h + 1] - log_rows[h : h + 1, u]
                mask = jnp.exp(gap)
                if q == r:
                    mask = jnp.where(causal, jnp.exp(jnp.where(causal, gap, 0.0)), 0.0)
                weights = (scores * mask).astype(BF16)
                mixed[t, lanes] += nn(weights, v_all[u, lanes])
                grown = nn(dy_t[lanes, t], weights)
                dv_t[h][r] = grown if dv_t[h][r] is None else dv_t[h][r] + grown
                score_grad = score_grad + nt(dy_all[t, lanes], v_all[u, lanes]) * mask
            score_grad = score_grad.astype(BF16)
            c_part = nn(score_grad, keys[u, :])
            b_part = tn(score_grad, queries[t, :])
            if r == 0:
                grad_c[t, :] = c_part
            else:
                grad_c[t, :] += c_part
            if q == r:
                grad_b[u, :] = b_part
            else:
                grad_b[u, :] += b_part
    whole_t = jnp.concatenate([jnp.concatenate(parts, axis=1) for parts in dv_t], axis=0)
    grad_v[...] = jnp.transpose(whole_t) + dy_wide * skip[...]


def carry_kernel(dims, where, mixed, grad_v, grad_c, grad_b, v_tail, dy_head, keys, queries, cols, carried, returned, *refs):
    g, rows, tiles, heads = dims
    pieces, (mixed_all, grad_v_all, grad_c_all, grad_b_all) = refs[:g], refs[g:]
    window = g * rows
    mine = where[0]
    log_cols = cols[:, :heads]
    head_decay = spread(jnp.exp(log_cols), heads, tiles)
    tail_decay = spread(jnp.exp(log_cols[window - 1 : window, :] - log_cols), heads, tiles)
    state = carried[...].astype(BF16)
    state_grad = returned[...].astype(BF16)
    mixed_all[...] = mixed[...] + head_decay * nn(queries[...], state)
    grad_v_all[...] = grad_v[...] + tail_decay * nn(keys[...], state_grad)
    grad_c_all[...] = grad_c[...] + nt(dy_head[...], state)
    grad_b_all[...] = grad_b[...] + nt(v_tail[...], state_grad)
    for d in range(g):
        piece = pieces[d]
        here = rows_of(lax.bitwise_xor(mine, d), rows)
        for k in range(tiles):
            lanes = slice(k * LANES, (k + 1) * LANES)
            piece[k * rows : (k + 1) * rows, :] = mixed_all[here, lanes]
            piece[(tiles + k) * rows : (tiles + k + 1) * rows, :] = grad_v_all[here, lanes]
        piece[2 * tiles * rows : (2 * tiles + 1) * rows, :] = grad_b_all[here, :]
        piece[(2 * tiles + 1) * rows : (2 * tiles + 2) * rows, :] = grad_c_all[here, :]


def unpack_kernel(dims, seqs, peers, where, *refs):
    g, rows, tiles, heads = dims
    pieces, refs = refs[: g * seqs], refs[g * seqs :]
    mixed, grad_v, shares, total = refs[0], refs[1], refs[2 : 2 + peers], refs[2 + peers]
    mine, core = where[0], where[1]
    for s in range(seqs):
        for d in range(g):
            piece = pieces[s * g + d]
            come = lax.bitwise_xor(mine, d)
            for k in range(tiles):
                lanes = pl.ds(pl.multiple_of((come * tiles + k) * LANES, LANES), LANES)
                mixed[s, :, lanes] = piece[k * rows : (k + 1) * rows, :].astype(BF16)
                grad_v[s, :, lanes] = piece[(tiles + k) * rows : (tiles + k + 1) * rows, :].astype(BF16)
        for w in range(2):
            at = slice((2 * tiles + w) * rows, (2 * tiles + w + 1) * rows)
            summed = pieces[s * g][at, :]
            for d in range(1, g):
                summed = summed + pieces[s * g + d][at, :]
            total[w, s] = summed
    part = rows // peers
    for e in range(peers):
        here = rows_of(lax.bitwise_xor(core, e), part)
        for s in range(seqs):
            for w in range(2):
                shares[e][w, s] = total[w, s, here, :]


def shards(values, keys_b, queries_c, forget, skip, cotangent):
    seqs, rows, wide = values.shape
    head_count = skip.shape[0]
    head_width = wide // head_count
    state_size = keys_b.shape[-1]
    blocks = lax.axis_size("seq")
    peers = lax.axis_size("head")
    g = max(1, min(8, wide // LANES, blocks))
    windows = blocks // g
    heads = head_count // g
    tiles = wide // g // LANES
    dims = (g, rows, tiles, heads)
    window = g * rows
    width = tiles * LANES
    index = lax.axis_index("seq")
    core = lax.axis_index("head")
    where = jnp.stack([lax.rem(index, g), core]).astype(jnp.int32)
    smem = pl.BlockSpec(memory_space=pltpu.SMEM)
    vmem = pl.BlockSpec(memory_space=pltpu.VMEM)

    def exchange(piece, d):
        if d == 0:
            return piece
        return lax.ppermute(piece, "seq", [(i, i ^ d) for i in range(blocks)])

    def shape(*dims, dtype=F32):
        return jax.ShapeDtypeStruct(dims, dtype)

    def call(kernel, out, ins, scratch=()):
        return pl.pallas_call(
            kernel,
            out_shape=out,
            in_specs=[smem] + [vmem] * (len(ins) - 1),
            out_specs=jax.tree.map(lambda _: vmem, out),
            scratch_shapes=list(scratch),
            compiler_params=VMEM,
        )(*ins)

    sent_rows = (2 * tiles + 2) * rows + 8
    back_rows = (2 * tiles + 2) * rows
    skip_part = lax.dynamic_slice(skip, (lax.rem(index, g) * heads,), (heads,))
    skip_row = jnp.repeat(skip_part, head_width)[None, :]
    got = []
    for s in range(seqs):
        pieces = call(
            functools.partial(pack_kernel, dims),
            [shape(sent_rows, LANES)] * g,
            [where, values[s], cotangent[s], keys_b[s], queries_c[s], forget[s]],
        )
        got.append([exchange(piece, d) for d, piece in enumerate(pieces)])
    back = []
    for s in range(seqs):
        (mixed, grad_v, grad_c, grad_b, v_tail, dy_head, keys, queries, cols, ahead, behind, decay) = call(
            functools.partial(local_kernel, dims),
            [
                shape(window, width),
                shape(window, width),
                shape(window, state_size),
                shape(window, state_size),
                shape(window, width, dtype=BF16),
                shape(window, width, dtype=BF16),
                shape(window, state_size, dtype=BF16),
                shape(window, state_size, dtype=BF16),
                shape(window, LANES),
                shape(state_size, width),
                shape(state_size, width),
                shape(8, width),
            ],
            [where, skip_row] + got[s],
            [
                pltpu.VMEM((window, width), BF16),
                pltpu.VMEM((window, width), BF16),
                pltpu.VMEM((g, 8, LANES), F32),
            ],
        )
        carried = jnp.zeros_like(ahead)
        returned = jnp.zeros_like(behind)
        rise = [(i, i + g) for i in range(blocks - g)]
        fall = [(i + g, i) for i in range(blocks - g)]
        for k in range(windows - 1):
            up = ahead if k == 0 else decay[:1] * carried + ahead
            down = behind if k == 0 else decay[:1] * returned + behind
            carried = lax.ppermute(up, "seq", rise)
            returned = lax.ppermute(down, "seq", fall)
        pieces = call(
            functools.partial(carry_kernel, dims),
            [shape(back_rows, LANES)] * g,
            [where, mixed, grad_v, grad_c, grad_b, v_tail, dy_head, keys, queries, cols, carried, returned],
            [pltpu.VMEM((window, width), F32)] * 2 + [pltpu.VMEM((window, state_size), F32)] * 2,
        )
        back.append([exchange(piece, d) for d, piece in enumerate(pieces)])
    part = rows // peers
    outs = call(
        functools.partial(unpack_kernel, dims, seqs, peers),
        [shape(seqs, rows, wide, dtype=BF16)] * 2 + [shape(2, seqs, part, state_size)] * peers,
        [where] + [piece for pieces in back for piece in pieces],
        [pltpu.VMEM((2, seqs, rows, state_size), F32)],
    )
    grad_bc = outs[2]
    for e in range(1, peers):
        grad_bc = grad_bc + lax.ppermute(outs[2 + e], "head", [(c, c ^ e) for c in range(peers)])
    return outs[0], outs[1], grad_bc


def solution(mesh):
    in_specs = (
        P(None, "seq", "head"),
        P(None, "seq", None),
        P(None, "seq", None),
        P(None, "head", "seq"),
        P("head"),
        P(None, "seq", "head"),
    )
    out_specs = (
        P(None, "seq", "head"),
        P(None, "seq", "head"),
        P(None, None, ("seq", "head"), None),
    )
    return jax.shard_map(shards, mesh=mesh, in_specs=in_specs, out_specs=out_specs, check_vma=False)
```

```python
import functools

import jax
import jax.numpy as jnp
from jax import lax
from jax.experimental import pallas as pl
from jax.experimental.pallas import tpu as pltpu
from jax.sharding import PartitionSpec as P

F32, BF16 = jnp.float32, jnp.bfloat16
LANES = 128
EXTRA = 8
MIB = 1024 * 1024


def nn(a, b):
    return lax.dot_general(a, b, (((1,), (0,)), ((), ())), preferred_element_type=F32)


def nt(a, b):
    return lax.dot_general(a, b, (((1,), (1,)), ((), ())), preferred_element_type=F32)


def tn(a, b):
    return lax.dot_general(a, b, (((0,), (0,)), ((), ())), preferred_element_type=F32)


def rows_of(block, rows):
    return pl.ds(pl.multiple_of(block * rows, rows), rows)


def partners(g):
    order = [0]
    for d in range(g // 2, g - 1):
        order += [d, g - 1 - d]
    return order + [g - 1] * (g > 1)


def place(g):
    index = lax.axis_index("seq")
    return lax.rem(index, g), lax.rem(lax.axis_index("head"), 2), lax.div(index, g)


def pick(flag, one, zero):
    if isinstance(flag, bool):
        return one if flag else zero
    return jnp.where(flag, one, zero)


def spread(columns, heads, tiles):
    per = heads // tiles
    width = LANES // per
    lane = lax.broadcasted_iota(jnp.int32, (columns.shape[0], LANES), 1)
    out = []
    for k in range(tiles):
        wide = jnp.broadcast_to(columns[:, k * per : k * per + 1], lane.shape)
        for e in range(1, per):
            h = k * per + e
            wide = jnp.where(lane >= e * width, columns[:, h : h + 1], wide)
        out.append(wide)
    return jnp.concatenate(out, axis=1) if tiles > 1 else out[0]


def pack_kernel(dims, shared, values, cotangent, keys, queries, forget, skip, *refs):
    g, rows, tiles, heads = dims
    pieces, (v_now, dy_now, b_now, c_now, f_now, s_now, arrived) = refs[:g], refs[g:]
    mine, core, _ = place(g)
    seq = core if shared else 1 - core
    half = values.shape[2] // 2
    moves = [(forget.at[seq], f_now), (skip, s_now)]
    if shared:
        moves += [(keys.at[seq], b_now), (queries.at[seq], c_now)]
    for whole, now in ((values, v_now), (cotangent, dy_now)):
        for k in range(2):
            lanes = pl.ds(k * half, half)
            moves.append((whole.at[seq, :, lanes], now.at[:, lanes]))
    copies = [pltpu.make_async_copy(a, b, arrived.at[n]) for n, (a, b) in enumerate(moves)]
    for copy in copies:
        copy.start()
    upto = lax.broadcasted_iota(jnp.int32, (rows, rows), 0) <= lax.broadcasted_iota(
        jnp.int32, (rows, rows), 1
    )
    for copy in copies:
        copy.wait()
    count = skip.shape[1]
    own = lax.broadcasted_iota(jnp.int32, (count, count), 0) == lax.broadcasted_iota(
        jnp.int32, (count, count), 1
    )
    skips = jnp.sum(jnp.where(own, s_now[...], 0.0), axis=1, keepdims=True)
    logcum = -lax.dot_general(
        f_now[...],
        upto.astype(F32),
        (((1,), (0,)), ((), ())),
        precision=lax.Precision.HIGHEST,
        preferred_element_type=F32,
    )
    held = jnp.concatenate([logcum, jnp.broadcast_to(skips, logcum.shape)], axis=1)
    for piece, d in zip(pieces, partners(g)):
        to = lax.bitwise_xor(mine, d)
        for k in range(tiles):
            lanes = pl.ds(pl.multiple_of((to * tiles + k) * LANES, LANES), LANES)
            piece[k * rows : (k + 1) * rows, :] = v_now[:, lanes].astype(F32)
            piece[(tiles + k) * rows : (tiles + k + 1) * rows, :] = dy_now[:, lanes].astype(F32)
        part = held[:heads]
        for j in range(1, g):
            part = jnp.where(to == j, held[j * heads : (j + 1) * heads], part)
        end = 2 * tiles * rows
        piece[end : end + heads, :] = part
        if heads < EXTRA:
            piece[end + heads : end + EXTRA, :] = jnp.zeros((EXTRA - heads, LANES), F32)
        if shared:
            piece[end + EXTRA : end + EXTRA + rows, :] = b_now[...].astype(F32)
            piece[end + EXTRA + rows : end + EXTRA + 2 * rows, :] = c_now[...].astype(F32)


def gather_kernel(dims, shared, *refs):
    g, rows, tiles, heads = dims
    pieces, refs = refs[:g], refs[g:]
    if shared:
        v_all, dy_all, log_rows, skip_row, keys, queries = refs[:6]
    else:
        keys, queries, v_all, dy_all, log_rows, skip_row = refs[:6]
    v_tail, dy_head, first, second, decay, blocks = refs[6:]
    window = g * rows
    mine, _, at_window = place(g)
    end = 2 * tiles * rows
    for piece, d in zip(pieces, partners(g)):
        at = lax.bitwise_xor(mine, d)
        here = rows_of(at, rows)
        for k in range(tiles):
            lanes = slice(k * LANES, (k + 1) * LANES)
            v_all[here, lanes] = piece[k * rows : (k + 1) * rows, :].astype(BF16)
            dy_all[here, lanes] = piece[(tiles + k) * rows : (tiles + k + 1) * rows, :].astype(BF16)
        blocks[at] = piece[end : end + EXTRA, :]
        if shared:
            keys[here, :] = piece[end + EXTRA : end + EXTRA + rows, :].astype(BF16)
            queries[here, :] = piece[end + EXTRA + rows : end + EXTRA + 2 * rows, :].astype(BF16)
    before = jnp.zeros((EXTRA, 1), F32)
    parts = []
    for j in range(g):
        block = blocks[j][:, :rows] + before
        before = block[:, rows - 1 : rows]
        parts.append(block)
    logs = jnp.concatenate(parts, axis=1)
    log_rows[...] = logs
    cols = jnp.transpose(logs)[:, :heads]
    skips = jnp.transpose(blocks[0])[rows : rows + 1, :heads]
    skip_row[...] = jnp.broadcast_to(spread(skips, heads, tiles), skip_row.shape)
    last = cols[window - 1 : window, :]
    v_tail[...] = (v_all[...].astype(F32) * spread(jnp.exp(last - cols), heads, tiles)).astype(BF16)
    dy_head[...] = (dy_all[...].astype(F32) * spread(jnp.exp(cols), heads, tiles)).astype(BF16)
    ahead = tn(keys[...], v_tail[...])
    behind = tn(queries[...], dy_head[...])
    odd = lax.rem(at_window, 2) == 1
    first[...] = jnp.where(odd, behind, ahead)
    second[...] = jnp.where(odd, ahead, behind)
    decay[...] = jnp.broadcast_to(spread(jnp.exp(last), heads, tiles), decay.shape)


def local_kernel(dims, v_all, dy_all, log_rows, skip_row, keys, queries, mixed, grad_v, grad_b, grad_c):
    g, rows, tiles, heads = dims
    window = g * rows
    head_width = tiles * LANES // heads
    log_cols = jnp.transpose(log_rows[...])[:, :heads]
    skips = skip_row[:1, :]
    mixed[...] = v_all[...].astype(F32) * skips
    dy_t = jnp.transpose(dy_all[...])
    tile = min(window, 256)
    causal = lax.broadcasted_iota(jnp.int32, (tile, tile), 0) >= lax.broadcasted_iota(
        jnp.int32, (tile, tile), 1
    )
    count = window // tile
    dv_t = [[None] * count for _ in range(heads)]
    for q in range(count):
        t = slice(q * tile, (q + 1) * tile)
        for r in range(q + 1):
            u = slice(r * tile, (r + 1) * tile)
            scores = nt(queries[t, :], keys[u, :])
            score_grad = jnp.zeros((tile, tile), F32)
            for h in range(heads):
                lanes = slice(h * head_width, (h + 1) * head_width)
                gap = log_cols[t, h : h + 1] - log_rows[h : h + 1, u]
                if q == r:
                    mask = jnp.where(causal, jnp.exp(jnp.where(causal, gap, 0.0)), 0.0)
                else:
                    mask = jnp.exp(gap)
                weights = (scores * mask).astype(BF16)
                mixed[t, lanes] += nn(weights, v_all[u, lanes])
                grown = nn(dy_t[lanes, t], weights)
                dv_t[h][r] = grown if dv_t[h][r] is None else dv_t[h][r] + grown
                score_grad = score_grad + nt(dy_all[t, lanes], v_all[u, lanes]) * mask
            score_grad = score_grad.astype(BF16)
            c_part = nn(score_grad, keys[u, :])
            b_part = tn(score_grad, queries[t, :])
            if r == 0:
                grad_c[t, :] = c_part
            else:
                grad_c[t, :] += c_part
            if q == r:
                grad_b[u, :] = b_part
            else:
                grad_b[u, :] += b_part
    whole_t = jnp.concatenate([jnp.concatenate(parts, axis=1) for parts in dv_t], axis=0)
    grad_v[...] = jnp.transpose(whole_t) + dy_all[...].astype(F32) * skips


def step_kernel(decay, state, total, moved):
    moved[...] = decay[:1, :] * state[...] + total[...]


def halves_of(dims, windows, half):
    _, _, at = place(dims[0])
    if windows != 4:
        return half == 0, None
    low = at < 2
    return (low if half == 0 else at >= 2), (at == 1) | (at == 2)


def half_kernel(dims, windows, half, last_part, log_rows, mixed, grad_v, grad_b, grad_c, *refs):
    g, rows, tiles, heads = dims
    if last_part:
        other, refs = refs[0], refs[1:]
    keys, queries, v_tail, dy_head, refs = *refs[:4], refs[4:]
    states, refs = refs[: len(refs) - g - 2], refs[len(refs) - g - 2 :]
    pieces, total, whole = refs[:g], refs[g], refs[g + 1]
    window = g * rows
    mine, _, _ = place(g)
    forward, inner = halves_of(dims, windows, half)
    if inner is None:
        state = states[0][...]
    elif half == 0:
        state = jnp.where(inner, states[0][...], 0.0)
    else:
        state = jnp.where(inner, states[0][...], states[1][...])
    state = state.astype(BF16)
    cols = jnp.transpose(log_rows[...])[:, :heads]
    last = cols[window - 1 : window, :]
    gain = spread(jnp.exp(pick(forward, cols, last - cols)), heads, tiles)
    more = gain * nn(pick(forward, queries[...], keys[...]), state)
    whole[...] = pick(forward, mixed[...], grad_v[...]) + more
    summed = pick(forward, grad_c[...], grad_b[...]) + nt(pick(forward, dy_head[...], v_tail[...]), state)
    if last_part:
        summed = summed + other[...]
    total[...] = summed
    for piece, d in zip(pieces, partners(g)):
        here = rows_of(lax.bitwise_xor(mine, d), rows)
        for k in range(tiles):
            piece[k * rows : (k + 1) * rows, :] = whole[here, k * LANES : (k + 1) * LANES]
        if last_part:
            piece[tiles * rows : (tiles + 1) * rows, :] = total[here, :]


def unpack_kernel(dims, windows, half, last_part, *refs):
    g, rows, tiles, heads = dims
    pieces, refs = refs[:g], refs[g:]
    if last_part or half:
        refs = refs[2:]
    mixed, grad_v, *shares, now, sent = refs
    if last_part:
        shares, total = shares[:-1], shares[-1]
    mine, core, _ = place(g)
    seq = 1 - core if last_part else core
    forward, _ = halves_of(dims, windows, half)
    for piece, d in zip(pieces, partners(g)):
        come = lax.bitwise_xor(mine, d)
        for k in range(tiles):
            lanes = pl.ds(pl.multiple_of((come * tiles + k) * LANES, LANES), LANES)
            now[:, lanes] = piece[k * rows : (k + 1) * rows, :].astype(BF16)

    def send(whole):
        part = now.shape[1] // 4
        copies = []
        for k in range(4):
            lanes = pl.ds(k * part, part)
            copies.append(pltpu.make_async_copy(now.at[:, lanes], whole.at[seq, :, lanes], sent.at[k]))
        for copy in copies:
            copy.start()
        for copy in copies:
            copy.wait()

    if isinstance(forward, bool):
        send(mixed if forward else grad_v)
    else:
        pl.when(forward)(lambda: send(mixed))
        pl.when(jnp.logical_not(forward))(lambda: send(grad_v))
    if last_part:
        at = slice(tiles * rows, (tiles + 1) * rows)
        total[...] = functools.reduce(jnp.add, [piece[at, :] for piece in pieces])
        for e, share in enumerate(shares):
            part = rows // len(shares)
            share[...] = total[rows_of(lax.bitwise_xor(lax.axis_index("head"), e), part), :]


def shards(values, keys_b, queries_c, forget, skip, cotangent):
    seqs, rows, wide = values.shape
    head_count = skip.shape[0]
    state_size = keys_b.shape[-1]
    blocks = lax.axis_size("seq")
    peers = lax.axis_size("head")
    g = max(1, min(4, wide // LANES, blocks))
    windows = blocks // g
    heads = head_count // g
    tiles = wide // g // LANES
    dims = (g, rows, tiles, heads)
    window = g * rows
    width = tiles * LANES
    index = lax.axis_index("seq")
    vmem = pl.BlockSpec(memory_space=pltpu.VMEM)

    def swap(send, pieces):
        return [send(piece, d) for d, piece in zip(partners(g), pieces)]

    def same(piece, d):
        if d == 0:
            return piece
        return lax.ppermute(piece, "seq", [(i, i ^ d) for i in range(blocks)])

    def cross(piece, d):
        perm = [
            (i * peers + c, (i ^ d) * peers + (c ^ 1)) for i in range(blocks) for c in range(peers)
        ]
        return lax.ppermute(piece, ("seq", "head"), perm)

    def shape(*dims, dtype=F32):
        return jax.ShapeDtypeStruct(dims, dtype)

    hbm = pl.BlockSpec(memory_space=pltpu.HBM)

    def call(kernel, out, ins, scratch=(), after=(), far=(), far_out=(), aliases={}, limit=48):
        count, extra = len(ins), len(after)

        def body(*refs):
            kernel(*refs[:count], *refs[count + extra :])

        outs = pl.pallas_call(
            body,
            out_shape=out,
            in_specs=[hbm if n in far else vmem for n in range(count)] + [hbm] * extra,
            out_specs=[hbm if n in far_out else vmem for n in range(len(out))],
            scratch_shapes=list(scratch),
            input_output_aliases=aliases,
            compiler_params=pltpu.CompilerParams(vmem_limit_bytes=limit * MIB),
        )(*ins, *after)
        return list(outs)

    base = 2 * tiles * rows
    got = []
    for shared in (True, False):
        pieces = call(
            functools.partial(pack_kernel, dims, shared),
            [shape(base + EXTRA + (2 * rows if shared else 0), LANES)] * g,
            [values, cotangent, keys_b, queries_c, forget, skip[None, :]],
            [
                pltpu.VMEM((rows, wide), BF16),
                pltpu.VMEM((rows, wide), BF16),
                pltpu.VMEM((rows, state_size), BF16),
                pltpu.VMEM((rows, state_size), BF16),
                pltpu.VMEM((head_count, rows), F32),
                pltpu.VMEM((1, head_count), F32),
                pltpu.SemaphoreType.DMA((8,)),
            ],
            after=[] if shared else got[0][1:2],
            far=range(6),
            limit=62 if shared else 48,
        )
        got.append(swap(same if shared else cross, pieces))
    rise = [(i, i + g) for i in range(blocks - g)]
    fall = [(i + g, i) for i in range(blocks - g)]
    map_shapes = [shape(window, state_size, dtype=BF16)] * 2
    own_shapes = [
        shape(window, width, dtype=BF16),
        shape(window, width, dtype=BF16),
        shape(EXTRA, window),
        shape(8, width),
    ]
    state_shape = shape(state_size, width)
    near = [(i, i ^ g) for i in range(blocks)]
    middle = [(i, i ^ (3 * g) if i // g in (1, 2) else i) for i in range(blocks)]
    maps, sums, back = [], {}, {}
    own, weighted, ends, state, results = ({} for _ in range(5))

    def gather(n, after=()):
        outs = call(
            functools.partial(gather_kernel, dims, n == 0),
            own_shapes
            + (map_shapes if n == 0 else [])
            + [shape(window, width, dtype=BF16)] * 2
            + [state_shape] * 2
            + [shape(8, width)],
            got[n] + maps,
            [pltpu.VMEM((g, EXTRA, LANES), F32)],
            after=after,
        )
        own[n], outs = outs[:4], outs[4:]
        if n == 0:
            maps.extend(outs[:2])
            outs = outs[2:]
        weighted[n], ends[n] = outs[:2], outs[2:]

    def local(n, after=()):
        results[n] = call(
            functools.partial(local_kernel, dims),
            [shape(window, width)] * 2 + [shape(window, state_size)] * 2,
            own[n] + maps,
            after=after,
        )

    def hop(n, k, after=()):
        first, second, decay = ends[n]
        if k == 0:
            state[n] = [lax.ppermute(first, "seq", near)]
            return []
        moved = call(
            step_kernel, [state_shape], [decay, state[n][-1], second if k == 1 else first], after=after
        )
        state[n].append(lax.ppermute(moved[0], "seq", middle if k == 1 else near))
        return moved

    def chain(n):
        first, second, decay = ends[n]
        odd = lax.rem(lax.div(index, g), 2) == 1
        total = [jnp.where(odd, second, first), jnp.where(odd, first, second)]
        state[n] = [jnp.zeros_like(first)] * 2
        for k in range(windows - 1):
            moved = [decay[:1] * a + b for a, b in zip(state[n], total)]
            state[n] = [lax.ppermute(moved[0], "seq", rise), lax.ppermute(moved[1], "seq", fall)]

    def finish(n, half, after=()):
        if windows == 4:
            states = state[n][:1] if half == 0 else state[n][1:]
        else:
            states = state[n][half : half + 1]
        outs = call(
            functools.partial(half_kernel, dims, windows, half, n == 1),
            [shape((tiles + n) * rows, LANES)] * g + [shape(window, state_size)],
            [own[n][2]] + results[n] + (sums[half] if n else []) + maps + weighted[n] + states,
            [pltpu.VMEM((window, width), F32)],
            after=after,
        )
        sums[half] = outs[g:]
        back[n, half] = swap(cross if n else same, outs[:g])

    gather(0)
    if windows == 4:
        hop(0, 0)
        local(0)
        moved = hop(0, 1, after=results[0][:1])
        finish(0, 0, after=moved)
        gather(1, after=sums[0])
        hop(1, 0)
        moved = hop(0, 2, after=ends[1][:1])
        local(1, after=moved)
        moved = hop(1, 1, after=results[1][:1])
        finish(1, 0, after=moved)
        finish(0, 1, after=sums[0])
        hop(1, 2, after=sums[1])
        finish(1, 1)
    else:
        gather(1)
        for n in range(2):
            chain(n)
            local(n)
            finish(n, 0)
            finish(n, 1)
    part = rows // peers
    outs, slices = [], []
    for n, half in ((0, 0), (1, 0), (0, 1), (1, 1)):
        more = [shape(part, state_size)] * peers if n else []
        outs = call(
            functools.partial(unpack_kernel, dims, windows, half, n == 1),
            [shape(seqs, rows, wide, dtype=BF16)] * 2 + more,
            back[n, half] + outs,
            [pltpu.VMEM((rows, state_size), F32)] * n
            + [pltpu.VMEM((rows, wide), BF16), pltpu.SemaphoreType.DMA((4,))],
            far=(g, g + 1),
            far_out=(0, 1),
            aliases={g: 0, g + 1: 1} if outs else {},
        )
        outs, shares = outs[:2], outs[2:]
        if n:
            come = [lax.ppermute(shares[e], "head", [(c, c ^ e) for c in range(peers)]) for e in range(1, peers)]
            ours = functools.reduce(jnp.add, come[1::2], shares[0])
            theirs = functools.reduce(jnp.add, come[2::2], come[0])
            even = lax.rem(lax.axis_index("head"), 2) == 0
            slices.append((jnp.where(even, theirs, ours), jnp.where(even, ours, theirs)))
    mixed, grad_v = outs
    low = lax.div(index, g) < 2 if windows == 4 else True
    grad_bc = jnp.stack(
        [jnp.stack([pick(low, a, b) for a, b in zip(*order)]) for order in (slices[::-1], slices)]
    )
    return mixed, grad_v, grad_bc


def solution(mesh):
    in_specs = (
        P(None, "seq", "head"),
        P(None, "seq", None),
        P(None, "seq", None),
        P(None, "head", "seq"),
        P("head"),
        P(None, "seq", "head"),
    )
    out_specs = (
        P(None, "seq", "head"),
        P(None, "seq", "head"),
        P(None, None, ("seq", "head"), None),
    )
    return jax.shard_map(shards, mesh=mesh, in_specs=in_specs, out_specs=out_specs, check_vma=False)
```

```python
import functools

import jax
import jax.numpy as jnp
from jax import lax
from jax.experimental import pallas as pl
from jax.experimental.pallas import tpu as pltpu
from jax.sharding import PartitionSpec as P

F32, BF16 = jnp.float32, jnp.bfloat16
LANES = 128
EXTRA = 8
MIB = 1024 * 1024


def nn(a, b):
    return lax.dot_general(a, b, (((1,), (0,)), ((), ())), preferred_element_type=F32)


def nt(a, b):
    return lax.dot_general(a, b, (((1,), (1,)), ((), ())), preferred_element_type=F32)


def tn(a, b):
    return lax.dot_general(a, b, (((0,), (0,)), ((), ())), preferred_element_type=F32)


def rows_of(block, rows):
    return pl.ds(pl.multiple_of(block * rows, rows), rows)


def partners(g):
    return [0, 2, 1, 3] if g == 4 else list(range(g))


def place(g):
    index = lax.axis_index("seq")
    return lax.rem(index, g), lax.rem(lax.axis_index("head"), 2), lax.div(index, g)


def pick(flag, one, zero):
    if isinstance(flag, bool):
        return one if flag else zero
    return jnp.where(flag, one, zero)


def spread(columns, heads, tiles):
    per = heads // tiles
    width = LANES // per
    lane = lax.broadcasted_iota(jnp.int32, (columns.shape[0], LANES), 1)
    out = []
    for k in range(tiles):
        wide = jnp.broadcast_to(columns[:, k * per : k * per + 1], lane.shape)
        for e in range(1, per):
            h = k * per + e
            wide = jnp.where(lane >= e * width, columns[:, h : h + 1], wide)
        out.append(wide)
    return jnp.concatenate(out, axis=1) if tiles > 1 else out[0]


def pack_kernel(dims, shared, values, cotangent, keys, queries, forget, skip, *refs):
    g, rows, tiles, heads = dims
    pieces, (v_now, dy_now, b_now, c_now, f_now, s_now, arrived) = refs[:g], refs[g:]
    mine, core, _ = place(g)
    seq = core if shared else 1 - core
    half = values.shape[2] // 2
    moves = [(forget.at[seq], f_now), (skip, s_now)]
    if shared:
        moves += [(keys.at[seq], b_now), (queries.at[seq], c_now)]
    for whole, now in ((values, v_now), (cotangent, dy_now)):
        for k in range(2):
            lanes = pl.ds(k * half, half)
            moves.append((whole.at[seq, :, lanes], now.at[:, lanes]))
    copies = [pltpu.make_async_copy(a, b, arrived.at[n]) for n, (a, b) in enumerate(moves)]
    for copy in copies:
        copy.start()
    upto = lax.broadcasted_iota(jnp.int32, (rows, rows), 0) <= lax.broadcasted_iota(
        jnp.int32, (rows, rows), 1
    )
    for copy in copies:
        copy.wait()
    count = skip.shape[1]
    own = lax.broadcasted_iota(jnp.int32, (count, count), 0) == lax.broadcasted_iota(
        jnp.int32, (count, count), 1
    )
    skips = jnp.sum(jnp.where(own, s_now[...], 0.0), axis=1, keepdims=True)
    logcum = -lax.dot_general(
        f_now[...],
        upto.astype(F32),
        (((1,), (0,)), ((), ())),
        precision=lax.Precision.HIGHEST,
        preferred_element_type=F32,
    )
    held = jnp.concatenate([logcum, jnp.broadcast_to(skips, logcum.shape)], axis=1)
    for piece, d in zip(pieces, partners(g)):
        to = lax.bitwise_xor(mine, d)
        for k in range(tiles):
            lanes = pl.ds(pl.multiple_of((to * tiles + k) * LANES, LANES), LANES)
            piece[k * rows : (k + 1) * rows, :] = v_now[:, lanes].astype(F32)
            piece[(tiles + k) * rows : (tiles + k + 1) * rows, :] = dy_now[:, lanes].astype(F32)
        part = held[:heads]
        for j in range(1, g):
            part = jnp.where(to == j, held[j * heads : (j + 1) * heads], part)
        end = 2 * tiles * rows
        piece[end : end + heads, :] = part
        if heads < EXTRA:
            piece[end + heads : end + EXTRA, :] = jnp.zeros((EXTRA - heads, LANES), F32)
        if shared:
            piece[end + EXTRA : end + EXTRA + rows, :] = b_now[...].astype(F32)
            piece[end + EXTRA + rows : end + EXTRA + 2 * rows, :] = c_now[...].astype(F32)


def gather_kernel(dims, shared, *refs):
    g, rows, tiles, heads = dims
    pieces, refs = refs[:g], refs[g:]
    if shared:
        v_all, dy_all, log_rows, skip_row, keys, queries = refs[:6]
    else:
        keys, queries, v_all, dy_all, log_rows, skip_row = refs[:6]
    weighted, first, blocks = refs[6:]
    window = g * rows
    mine, _, at_window = place(g)
    end = 2 * tiles * rows
    for piece, d in zip(pieces, partners(g)):
        at = lax.bitwise_xor(mine, d)
        here = rows_of(at, rows)
        for k in range(tiles):
            lanes = slice(k * LANES, (k + 1) * LANES)
            v_all[here, lanes] = piece[k * rows : (k + 1) * rows, :].astype(BF16)
            dy_all[here, lanes] = piece[(tiles + k) * rows : (tiles + k + 1) * rows, :].astype(BF16)
        blocks[at] = piece[end : end + EXTRA, :]
        if shared:
            keys[here, :] = piece[end + EXTRA : end + EXTRA + rows, :].astype(BF16)
            queries[here, :] = piece[end + EXTRA + rows : end + EXTRA + 2 * rows, :].astype(BF16)
    before = jnp.zeros((EXTRA, 1), F32)
    parts = []
    for j in range(g):
        block = blocks[j][:, :rows] + before
        before = block[:, rows - 1 : rows]
        parts.append(block)
    logs = jnp.concatenate(parts, axis=1)
    log_rows[...] = logs
    cols = jnp.transpose(logs)[:, :heads]
    skips = jnp.transpose(blocks[0])[rows : rows + 1, :heads]
    skip_row[...] = jnp.broadcast_to(spread(skips, heads, tiles), skip_row.shape)
    last = cols[window - 1 : window, :]
    odd = lax.rem(at_window, 2) == 1
    gain = spread(jnp.exp(jnp.where(odd, cols, last - cols)), heads, tiles)
    weighted[...] = (jnp.where(odd, dy_all[...], v_all[...]).astype(F32) * gain).astype(BF16)
    states = first.shape[0] - EXTRA
    first[:states, :] = tn(jnp.where(odd, queries[...], keys[...]), weighted[...])
    first[states:, :] = jnp.broadcast_to(spread(jnp.exp(last), heads, tiles), (EXTRA, tiles * LANES))


def second_kernel(dims, v_all, dy_all, log_rows, keys, queries, weighted, second):
    g, rows, tiles, heads = dims
    _, _, at_window = place(g)
    odd = lax.rem(at_window, 2) == 1
    cols = jnp.transpose(log_rows[...])[:, :heads]
    last = cols[g * rows - 1 :, :]
    gain = spread(jnp.exp(jnp.where(odd, last - cols, cols)), heads, tiles)
    weighted[...] = (jnp.where(odd, v_all[...], dy_all[...]).astype(F32) * gain).astype(BF16)
    second[...] = tn(jnp.where(odd, keys[...], queries[...]), weighted[...])


def local_kernel(dims, v_all, dy_all, log_rows, skip_row, keys, queries, mixed, grad_v, grad_b, grad_c):
    g, rows, tiles, heads = dims
    window = g * rows
    head_width = tiles * LANES // heads
    log_cols = jnp.transpose(log_rows[...])[:, :heads]
    skips = skip_row[:1, :]
    mixed[...] = v_all[...].astype(F32) * skips
    dy_t = jnp.transpose(dy_all[...])
    tile = min(window, 256)
    causal = lax.broadcasted_iota(jnp.int32, (tile, tile), 0) >= lax.broadcasted_iota(
        jnp.int32, (tile, tile), 1
    )
    count = window // tile
    dv_t = [[None] * count for _ in range(heads)]
    for q in range(count):
        t = slice(q * tile, (q + 1) * tile)
        for r in range(q + 1):
            u = slice(r * tile, (r + 1) * tile)
            scores = nt(queries[t, :], keys[u, :])
            score_grad = jnp.zeros((tile, tile), F32)
            for h in range(heads):
                lanes = slice(h * head_width, (h + 1) * head_width)
                gap = log_cols[t, h : h + 1] - log_rows[h : h + 1, u]
                if q == r:
                    mask = jnp.where(causal, jnp.exp(jnp.where(causal, gap, 0.0)), 0.0)
                else:
                    mask = jnp.exp(gap)
                weights = (scores * mask).astype(BF16)
                mixed[t, lanes] += nn(weights, v_all[u, lanes])
                grown = nn(dy_t[lanes, t], weights)
                dv_t[h][r] = grown if dv_t[h][r] is None else dv_t[h][r] + grown
                score_grad = score_grad + nt(dy_all[t, lanes], v_all[u, lanes]) * mask
            score_grad = score_grad.astype(BF16)
            c_part = nn(score_grad, keys[u, :])
            b_part = tn(score_grad, queries[t, :])
            if r == 0:
                grad_c[t, :] = c_part
            else:
                grad_c[t, :] += c_part
            if q == r:
                grad_b[u, :] = b_part
            else:
                grad_b[u, :] += b_part
    whole_t = jnp.concatenate([jnp.concatenate(parts, axis=1) for parts in dv_t], axis=0)
    grad_v[...] = jnp.transpose(whole_t) + dy_all[...].astype(F32) * skips


def step_kernel(first, second, near, pair):
    states = pair.shape[0]
    pair[...] = first[states : states + 1, :] * near[:states, :] + second[...]


def last_kernel(first, far, moved):
    states = moved.shape[0]
    moved[...] = first[states : states + 1, :] * far[...] + first[:states, :]


def halves_of(dims, windows, half):
    _, _, at = place(dims[0])
    if windows != 4:
        return half == 0, None
    low = at < 2
    return (low if half == 0 else at >= 2), (at == 1) | (at == 2)


def half_kernel(dims, windows, half, last_part, doubled, log_rows, mixed, grad_v, grad_b, grad_c, *refs):
    g, rows, tiles, heads = dims
    if last_part:
        other, refs = refs[0], refs[1:]
    keys, queries, to_first, to_second, refs = *refs[:4], refs[4:]
    states, refs = refs[: len(refs) - g - 2], refs[len(refs) - g - 2 :]
    pieces, total, whole = refs[:g], refs[g], refs[g + 1]
    window = g * rows
    mine, _, at_window = place(g)
    forward, inner = halves_of(dims, windows, half)
    if inner is None:
        state = states[0][...]
    else:
        count = keys.shape[1]
        near = states[0][:count, :]
        if half == 0:
            state = jnp.where(inner, near, 0.0)
        else:
            outer = states[2][...]
            if doubled:
                outer = states[0][count : count + 1, :] * outer + near
            state = jnp.where(inner, states[1][...], outer)
    state = state.astype(BF16)
    cols = jnp.transpose(log_rows[...])[:, :heads]
    last = cols[window - 1 : window, :]
    gain = spread(jnp.exp(pick(forward, cols, last - cols)), heads, tiles)
    more = gain * nn(pick(forward, queries[...], keys[...]), state)
    whole[...] = pick(forward, mixed[...], grad_v[...]) + more
    odd = lax.rem(at_window, 2) == 1
    used = odd if forward is True else jnp.logical_not(odd) if forward is False else odd == forward
    summed = pick(forward, grad_c[...], grad_b[...]) + nt(jnp.where(used, to_first[...], to_second[...]), state)
    if last_part:
        summed = summed + other[...]
    total[...] = summed
    for piece, d in zip(pieces, partners(g)):
        here = rows_of(lax.bitwise_xor(mine, d), rows)
        for k in range(tiles):
            piece[k * rows : (k + 1) * rows, :] = whole[here, k * LANES : (k + 1) * LANES]
        if last_part:
            piece[tiles * rows : (tiles + 1) * rows, :] = total[here, :]


def sum_kernel(dims, *refs):
    g, rows, tiles, heads = dims
    pieces, shares, total = refs[:g], refs[g:-1], refs[-1]
    at = slice(tiles * rows, (tiles + 1) * rows)
    total[...] = functools.reduce(jnp.add, [piece[at, :] for piece in pieces])
    for e, share in enumerate(shares):
        part = rows // len(shares)
        share[...] = total[rows_of(lax.bitwise_xor(lax.axis_index("head"), e), part), :]


def unpack_kernel(dims, windows, half, last_part, *refs):
    g, rows, tiles, heads = dims
    pieces, refs = refs[:g], refs[g:]
    mixed, grad_v, done, now, sent = refs[-5:]
    done[...] = jnp.zeros_like(done)
    mine, core, _ = place(g)
    seq = 1 - core if last_part else core
    forward, _ = halves_of(dims, windows, half)
    for piece, d in zip(pieces, partners(g)):
        come = lax.bitwise_xor(mine, d)
        for k in range(tiles):
            lanes = pl.ds(pl.multiple_of((come * tiles + k) * LANES, LANES), LANES)
            now[:, lanes] = piece[k * rows : (k + 1) * rows, :].astype(BF16)

    def send(whole):
        part = now.shape[1] // 4
        copies = []
        for k in range(4):
            lanes = pl.ds(k * part, part)
            copies.append(pltpu.make_async_copy(now.at[:, lanes], whole.at[seq, :, lanes], sent.at[k]))
        for copy in copies:
            copy.start()
        for copy in copies:
            copy.wait()

    if isinstance(forward, bool):
        send(mixed if forward else grad_v)
    else:
        pl.when(forward)(lambda: send(mixed))
        pl.when(jnp.logical_not(forward))(lambda: send(grad_v))


def shards(values, keys_b, queries_c, forget, skip, cotangent):
    seqs, rows, wide = values.shape
    head_count = skip.shape[0]
    state_size = keys_b.shape[-1]
    blocks = lax.axis_size("seq")
    peers = lax.axis_size("head")
    g = max(1, min(4, wide // LANES, blocks))
    windows = blocks // g
    heads = head_count // g
    tiles = wide // g // LANES
    dims = (g, rows, tiles, heads)
    window = g * rows
    width = tiles * LANES
    index = lax.axis_index("seq")
    vmem = pl.BlockSpec(memory_space=pltpu.VMEM)

    def swap(send, pieces):
        return [send(piece, d) for d, piece in zip(partners(g), pieces)]

    def same(piece, d):
        if d == 0:
            return piece
        return lax.ppermute(piece, "seq", [(i, i ^ d) for i in range(blocks)])

    def cross(piece, d):
        perm = [
            (i * peers + c, (i ^ d) * peers + (c ^ 1)) for i in range(blocks) for c in range(peers)
        ]
        return lax.ppermute(piece, ("seq", "head"), perm)

    def shape(*dims, dtype=F32):
        return jax.ShapeDtypeStruct(dims, dtype)

    hbm = pl.BlockSpec(memory_space=pltpu.HBM)

    def call(kernel, out, ins, scratch=(), after=(), far=(), far_out=(), aliases={}, limit=48):
        count, extra = len(ins), len(after)

        def body(*refs):
            kernel(*refs[:count], *refs[count + extra :])

        outs = pl.pallas_call(
            body,
            out_shape=out,
            in_specs=[hbm if n in far else vmem for n in range(count)] + [hbm] * extra,
            out_specs=[hbm if n in far_out else vmem for n in range(len(out))],
            scratch_shapes=list(scratch),
            input_output_aliases=aliases,
            cost_estimate=pl.CostEstimate(
                flops=0,
                bytes_accessed=sum(a.size * a.dtype.itemsize for a in list(ins) + list(out)),
                transcendentals=0,
            ),
            compiler_params=pltpu.CompilerParams(vmem_limit_bytes=limit * MIB),
        )(*ins, *after)
        return list(outs)

    base = 2 * tiles * rows
    got = []
    for shared in (True, False):
        pieces = call(
            functools.partial(pack_kernel, dims, shared),
            [shape(base + EXTRA + (2 * rows if shared else 0), LANES)] * g,
            [values, cotangent, keys_b, queries_c, forget, skip[None, :]],
            [
                pltpu.VMEM((rows, wide), BF16),
                pltpu.VMEM((rows, wide), BF16),
                pltpu.VMEM((rows, state_size), BF16),
                pltpu.VMEM((rows, state_size), BF16),
                pltpu.VMEM((head_count, rows), F32),
                pltpu.VMEM((1, head_count), F32),
                pltpu.SemaphoreType.DMA((8,)),
            ],
            far=range(6),
            limit=62 if shared else 48,
        )
        got.append(swap(same if shared else cross, pieces))
    rise = [(i, i + g) for i in range(blocks - g)]
    fall = [(i + g, i) for i in range(blocks - g)]
    map_shapes = [shape(window, state_size, dtype=BF16)] * 2
    own_shapes = [
        shape(window, width, dtype=BF16),
        shape(window, width, dtype=BF16),
        shape(EXTRA, window),
        shape(8, width),
    ]
    state_shape = shape(state_size, width)
    near = [(i, i ^ g) for i in range(blocks)]
    middle = [(i, i ^ (3 * g) if i // g in (1, 2) else i) for i in range(blocks)]
    outer = [(i, i ^ (2 * g)) for i in range(blocks) if i // g in (1, 2)]
    maps, sums, back = [], {}, {}
    own, weighted, ends, state, results = ({} for _ in range(5))

    def gather(n, after=()):
        outs = call(
            functools.partial(gather_kernel, dims, n == 0),
            own_shapes
            + (map_shapes if n == 0 else [])
            + [shape(window, width, dtype=BF16), shape(state_size + EXTRA, width)],
            got[n] + maps,
            [pltpu.VMEM((g, EXTRA, LANES), F32)],
            after=after,
        )
        own[n], outs = outs[:4], outs[4:]
        if n == 0:
            maps.extend(outs[:2])
            outs = outs[2:]
        weighted[n], ends[n] = outs[:1], outs[1:]

    def second(n, after=()):
        outs = call(
            functools.partial(second_kernel, dims),
            [shape(window, width, dtype=BF16), state_shape],
            own[n][:3] + maps,
            after=after,
        )
        weighted[n] += outs[:1]
        ends[n] += outs[1:]

    def local(n, after=()):
        results[n] = call(
            functools.partial(local_kernel, dims),
            [shape(window, width)] * 2 + [shape(window, state_size)] * 2,
            own[n] + maps,
            after=after,
        )

    def meet(n):
        state[n] = [lax.ppermute(ends[n][0], "seq", near)]

    def cross_pairs(n, after=()):
        pair = call(step_kernel, [state_shape], ends[n] + state[n], after=after)
        state[n] += [lax.ppermute(pair[0], "seq", perm) for perm in (middle, outer)]
        return pair

    def step(n, k, after=()):
        first, other = ends[n]
        if k == 1:
            moved = call(step_kernel, [state_shape], [first, other, state[n][-1]], after=after)
        else:
            moved = call(last_kernel, [state_shape], [first, state[n][-1]], after=after)
        state[n].append(lax.ppermute(moved[0], "seq", middle if k == 1 else near))
        return moved

    def chain(n):
        first, other = ends[n]
        first, decay = first[:state_size], first[state_size : state_size + 1]
        odd = lax.rem(lax.div(index, g), 2) == 1
        total = [jnp.where(odd, other, first), jnp.where(odd, first, other)]
        state[n] = [jnp.zeros_like(first)] * 2
        for k in range(windows - 1):
            moved = [decay * a + b for a, b in zip(state[n], total)]
            state[n] = [lax.ppermute(moved[0], "seq", rise), lax.ppermute(moved[1], "seq", fall)]

    def finish(n, half, after=()):
        if windows == 4:
            states = state[n][:1] if half == 0 else state[n]
        else:
            states = state[n][half : half + 1]
        outs = call(
            functools.partial(half_kernel, dims, windows, half, n == 1, n == 1),
            [shape((tiles + n) * rows, LANES)] * g + [shape(window, state_size)],
            [own[n][2]] + results[n] + (sums[half] if n else []) + maps + weighted[n] + states,
            [pltpu.VMEM((window, width), F32)],
            after=after,
        )
        sums[half] = outs[g:]
        back[n, half] = swap(cross if n else same, outs[:g])

    gather(0)
    if windows == 4:
        meet(0)
        second(0)
        local(0)
        gather(1, after=results[0][:1])
        meet(1)
        second(1)
        moved = step(0, 1, after=ends[1][:1])
        finish(0, 0, after=moved)
        local(1)
        cross_pairs(1, after=back[0, 0][1:3] + state[0][1:] + results[1][:1])
        finish(1, 0)
        step(0, 2)
        finish(0, 1, after=back[1, 0][1:2])
        finish(1, 1, after=back[1, 0][2:] + back[0, 1][1:3])
    else:
        gather(1)
        for n in range(2):
            second(n)
            chain(n)
            local(n)
            finish(n, 0)
            finish(n, 1)
    part = rows // peers
    outs, slices, done = [], [], []
    for n, half in ((0, 0), (0, 1), (1, 0), (1, 1)):
        if n:
            shares = call(
                functools.partial(sum_kernel, dims),
                [shape(part, state_size)] * peers,
                back[n, half],
                [pltpu.VMEM((rows, state_size), F32)],
                after=done,
            )
        outs = call(
            functools.partial(unpack_kernel, dims, windows, half, n == 1),
            [shape(seqs, rows, wide, dtype=BF16)] * 2 + [shape(8, LANES)],
            back[n, half] + outs,
            [pltpu.VMEM((rows, wide), BF16), pltpu.SemaphoreType.DMA((4,))],
            far=(g, g + 1),
            far_out=(0, 1),
            aliases={g: 0, g + 1: 1} if outs else {},
        )
        outs, done = outs[:2], outs[2:]
        if n:
            come = [lax.ppermute(shares[e], "head", [(c, c ^ e) for c in range(peers)]) for e in range(1, peers)]
            ours = functools.reduce(jnp.add, come[1::2], shares[0])
            theirs = functools.reduce(jnp.add, come[2::2], come[0])
            even = lax.rem(lax.axis_index("head"), 2) == 0
            slices.append((jnp.where(even, theirs, ours), jnp.where(even, ours, theirs)))
    mixed, grad_v = outs
    low = lax.div(index, g) < 2 if windows == 4 else True
    grad_bc = jnp.stack(
        [jnp.stack([pick(low, a, b) for a, b in zip(*order)]) for order in (slices[::-1], slices)]
    )
    return mixed, grad_v, grad_bc


def solution(mesh):
    in_specs = (
        P(None, "seq", "head"),
        P(None, "seq", None),
        P(None, "seq", None),
        P(None, "head", "seq"),
        P("head"),
        P(None, "seq", "head"),
    )
    out_specs = (
        P(None, "seq", "head"),
        P(None, "seq", "head"),
        P(None, None, ("seq", "head"), None),
    )
    return jax.shard_map(shards, mesh=mesh, in_specs=in_specs, out_specs=out_specs, check_vma=False)
```

```python
import functools

import jax
import jax.numpy as jnp
from jax import lax
from jax.experimental import pallas as pl
from jax.experimental.pallas import tpu as pltpu
from jax.sharding import PartitionSpec as P

F32, BF16 = jnp.float32, jnp.bfloat16
LANES = 128
EXTRA = 8
MIB = 1024 * 1024


def nn(a, b):
    return lax.dot_general(a, b, (((1,), (0,)), ((), ())), preferred_element_type=F32)


def nt(a, b):
    return lax.dot_general(a, b, (((1,), (1,)), ((), ())), preferred_element_type=F32)


def tn(a, b):
    return lax.dot_general(a, b, (((0,), (0,)), ((), ())), preferred_element_type=F32)


def rows_of(block, rows):
    return pl.ds(pl.multiple_of(block * rows, rows), rows)


def partners(g):
    return [0, 2, 1, 3] if g == 4 else list(range(g))


def place(g):
    index = lax.axis_index("seq")
    return lax.rem(index, g), lax.rem(lax.axis_index("head"), 2), lax.div(index, g)


def pick(flag, one, zero):
    if isinstance(flag, bool):
        return one if flag else zero
    return jnp.where(flag, one, zero)


def spread(columns, heads, tiles):
    per = heads // tiles
    width = LANES // per
    lane = lax.broadcasted_iota(jnp.int32, (columns.shape[0], LANES), 1)
    out = []
    for k in range(tiles):
        wide = jnp.broadcast_to(columns[:, k * per : k * per + 1], lane.shape)
        for e in range(1, per):
            h = k * per + e
            wide = jnp.where(lane >= e * width, columns[:, h : h + 1], wide)
        out.append(wide)
    return jnp.concatenate(out, axis=1) if tiles > 1 else out[0]


def pack_kernel(dims, shared, values, cotangent, keys, queries, forget, skip, *refs):
    g, rows, tiles, heads = dims
    pieces, (v_now, dy_now, b_now, c_now, f_now, s_now, arrived) = refs[:g], refs[g:]
    mine, core, _ = place(g)
    seq = core if shared else 1 - core
    half = values.shape[2] // 2
    moves = [(forget.at[seq], f_now), (skip, s_now)]
    if shared:
        moves += [(keys.at[seq], b_now), (queries.at[seq], c_now)]
    for whole, now in ((values, v_now), (cotangent, dy_now)):
        for k in range(2):
            lanes = pl.ds(k * half, half)
            moves.append((whole.at[seq, :, lanes], now.at[:, lanes]))
    copies = [pltpu.make_async_copy(a, b, arrived.at[n]) for n, (a, b) in enumerate(moves)]
    for copy in copies:
        copy.start()
    upto = lax.broadcasted_iota(jnp.int32, (rows, rows), 0) <= lax.broadcasted_iota(
        jnp.int32, (rows, rows), 1
    )
    for copy in copies:
        copy.wait()
    count = skip.shape[1]
    own = lax.broadcasted_iota(jnp.int32, (count, count), 0) == lax.broadcasted_iota(
        jnp.int32, (count, count), 1
    )
    skips = jnp.sum(jnp.where(own, s_now[...], 0.0), axis=1, keepdims=True)
    logcum = -lax.dot_general(
        f_now[...],
        upto.astype(F32),
        (((1,), (0,)), ((), ())),
        precision=lax.Precision.HIGHEST,
        preferred_element_type=F32,
    )
    held = jnp.concatenate([logcum, jnp.broadcast_to(skips, logcum.shape)], axis=1)
    for piece, d in zip(pieces, partners(g)):
        to = lax.bitwise_xor(mine, d)
        for k in range(tiles):
            lanes = pl.ds(pl.multiple_of((to * tiles + k) * LANES, LANES), LANES)
            piece[k * rows : (k + 1) * rows, :] = v_now[:, lanes].astype(F32)
            piece[(tiles + k) * rows : (tiles + k + 1) * rows, :] = dy_now[:, lanes].astype(F32)
        part = held[:heads]
        for j in range(1, g):
            part = jnp.where(to == j, held[j * heads : (j + 1) * heads], part)
        end = 2 * tiles * rows
        piece[end : end + heads, :] = part
        if heads < EXTRA:
            piece[end + heads : end + EXTRA, :] = jnp.zeros((EXTRA - heads, LANES), F32)
        if shared:
            piece[end + EXTRA : end + EXTRA + rows, :] = b_now[...].astype(F32)
            piece[end + EXTRA + rows : end + EXTRA + 2 * rows, :] = c_now[...].astype(F32)


def gather_kernel(dims, shared, *refs):
    g, rows, tiles, heads = dims
    pieces, refs = refs[:g], refs[g:]
    if shared:
        v_all, dy_all, log_rows, skip_row, keys, queries = refs[:6]
    else:
        keys, queries, v_all, dy_all, log_rows, skip_row = refs[:6]
    weighted, first, blocks = refs[6:]
    window = g * rows
    mine, _, at_window = place(g)
    end = 2 * tiles * rows
    for piece, d in zip(pieces, partners(g)):
        at = lax.bitwise_xor(mine, d)
        here = rows_of(at, rows)
        for k in range(tiles):
            lanes = slice(k * LANES, (k + 1) * LANES)
            v_all[here, lanes] = piece[k * rows : (k + 1) * rows, :].astype(BF16)
            dy_all[here, lanes] = piece[(tiles + k) * rows : (tiles + k + 1) * rows, :].astype(BF16)
        blocks[at] = piece[end : end + EXTRA, :]
        if shared:
            keys[here, :] = piece[end + EXTRA : end + EXTRA + rows, :].astype(BF16)
            queries[here, :] = piece[end + EXTRA + rows : end + EXTRA + 2 * rows, :].astype(BF16)
    before = jnp.zeros((EXTRA, 1), F32)
    parts = []
    for j in range(g):
        block = blocks[j][:, :rows] + before
        before = block[:, rows - 1 : rows]
        parts.append(block)
    logs = jnp.concatenate(parts, axis=1)
    log_rows[...] = logs
    cols = jnp.transpose(logs)[:, :heads]
    skips = jnp.transpose(blocks[0])[rows : rows + 1, :heads]
    skip_row[...] = jnp.broadcast_to(spread(skips, heads, tiles), skip_row.shape)
    last = cols[window - 1 : window, :]
    odd = lax.rem(at_window, 2) == 1
    gain = spread(jnp.exp(jnp.where(odd, cols, last - cols)), heads, tiles)
    weighted[...] = (jnp.where(odd, dy_all[...], v_all[...]).astype(F32) * gain).astype(BF16)
    states = first.shape[0] - EXTRA
    first[:states, :] = tn(jnp.where(odd, queries[...], keys[...]), weighted[...])
    first[states:, :] = jnp.broadcast_to(spread(jnp.exp(last), heads, tiles), (EXTRA, tiles * LANES))


def second_kernel(dims, v_all, dy_all, log_rows, keys, queries, weighted, second):
    g, rows, tiles, heads = dims
    _, _, at_window = place(g)
    odd = lax.rem(at_window, 2) == 1
    cols = jnp.transpose(log_rows[...])[:, :heads]
    last = cols[g * rows - 1 :, :]
    gain = spread(jnp.exp(jnp.where(odd, last - cols, cols)), heads, tiles)
    weighted[...] = (jnp.where(odd, v_all[...], dy_all[...]).astype(F32) * gain).astype(BF16)
    second[...] = tn(jnp.where(odd, keys[...], queries[...]), weighted[...])


def local_kernel(dims, v_all, dy_all, log_rows, skip_row, keys, queries, mixed, grad_v, grad_b, grad_c):
    g, rows, tiles, heads = dims
    window = g * rows
    head_width = tiles * LANES // heads
    log_cols = jnp.transpose(log_rows[...])[:, :heads]
    skips = skip_row[:1, :]
    mixed[...] = v_all[...].astype(F32) * skips
    dy_t = jnp.transpose(dy_all[...])
    tile = min(window, 256)
    causal = lax.broadcasted_iota(jnp.int32, (tile, tile), 0) >= lax.broadcasted_iota(
        jnp.int32, (tile, tile), 1
    )
    count = window // tile
    dv_t = [[None] * count for _ in range(heads)]
    for q in range(count):
        t = slice(q * tile, (q + 1) * tile)
        for r in range(q + 1):
            u = slice(r * tile, (r + 1) * tile)
            scores = nt(queries[t, :], keys[u, :])
            score_grad = jnp.zeros((tile, tile), F32)
            for h in range(heads):
                lanes = slice(h * head_width, (h + 1) * head_width)
                gap = log_cols[t, h : h + 1] - log_rows[h : h + 1, u]
                if q == r:
                    mask = jnp.where(causal, jnp.exp(jnp.where(causal, gap, 0.0)), 0.0)
                else:
                    mask = jnp.exp(gap)
                weights = (scores * mask).astype(BF16)
                mixed[t, lanes] += nn(weights, v_all[u, lanes])
                grown = nn(dy_t[lanes, t], weights)
                dv_t[h][r] = grown if dv_t[h][r] is None else dv_t[h][r] + grown
                score_grad = score_grad + nt(dy_all[t, lanes], v_all[u, lanes]) * mask
            score_grad = score_grad.astype(BF16)
            c_part = nn(score_grad, keys[u, :])
            b_part = tn(score_grad, queries[t, :])
            if r == 0:
                grad_c[t, :] = c_part
            else:
                grad_c[t, :] += c_part
            if q == r:
                grad_b[u, :] = b_part
            else:
                grad_b[u, :] += b_part
    whole_t = jnp.concatenate([jnp.concatenate(parts, axis=1) for parts in dv_t], axis=0)
    grad_v[...] = jnp.transpose(whole_t) + dy_all[...].astype(F32) * skips


def step_kernel(first, second, near, pair):
    states = pair.shape[0]
    pair[...] = first[states : states + 1, :] * near[:states, :] + second[...]


def last_kernel(first, far, moved):
    states = moved.shape[0]
    moved[...] = first[states : states + 1, :] * far[...] + first[:states, :]


def halves_of(dims, windows, half):
    _, _, at = place(dims[0])
    if windows != 4:
        return half == 0, None
    low = at < 2
    return (low if half == 0 else at >= 2), (at == 1) | (at == 2)


def half_kernel(dims, windows, half, last_part, doubled, log_rows, mixed, grad_v, grad_b, grad_c, *refs):
    g, rows, tiles, heads = dims
    if last_part:
        other, refs = refs[0], refs[1:]
    keys, queries, to_first, to_second, refs = *refs[:4], refs[4:]
    states, refs = refs[: len(refs) - g - 2], refs[len(refs) - g - 2 :]
    pieces, total, whole = refs[:g], refs[g], refs[g + 1]
    window = g * rows
    mine, _, at_window = place(g)
    forward, inner = halves_of(dims, windows, half)
    if inner is None:
        state = states[0][...]
    else:
        count = keys.shape[1]
        near = states[0][:count, :]
        if half == 0:
            state = jnp.where(inner, near, 0.0)
        else:
            outer = states[2][...]
            if doubled:
                outer = states[0][count : count + 1, :] * outer + near
            state = jnp.where(inner, states[1][...], outer)
    state = state.astype(BF16)
    cols = jnp.transpose(log_rows[...])[:, :heads]
    last = cols[window - 1 : window, :]
    gain = spread(jnp.exp(pick(forward, cols, last - cols)), heads, tiles)
    more = gain * nn(pick(forward, queries[...], keys[...]), state)
    whole[...] = pick(forward, mixed[...], grad_v[...]) + more
    odd = lax.rem(at_window, 2) == 1
    used = odd if forward is True else jnp.logical_not(odd) if forward is False else odd == forward
    summed = pick(forward, grad_c[...], grad_b[...]) + nt(jnp.where(used, to_first[...], to_second[...]), state)
    if last_part:
        summed = summed + other[...]
    total[...] = summed
    for piece, d in zip(pieces, partners(g)):
        here = rows_of(lax.bitwise_xor(mine, d), rows)
        for k in range(tiles):
            piece[k * rows : (k + 1) * rows, :] = whole[here, k * LANES : (k + 1) * LANES]
        if last_part:
            piece[tiles * rows : (tiles + 1) * rows, :] = total[here, :]


def sum_kernel(dims, *refs):
    g, rows, tiles, heads = dims
    pieces, shares, total = refs[:g], refs[g:-1], refs[-1]
    at = slice(tiles * rows, (tiles + 1) * rows)
    total[...] = functools.reduce(jnp.add, [piece[at, :] for piece in pieces])
    for e, share in enumerate(shares):
        part = rows // len(shares)
        share[...] = total[rows_of(lax.bitwise_xor(lax.axis_index("head"), e), part), :]


def unpack_kernel(dims, windows, half, last_part, marked, *refs):
    g, rows, tiles, heads = dims
    pieces, refs = refs[:g], refs[g:]
    mixed, grad_v, *done, now, sent = refs[-5:] if marked else refs[-4:]
    for mark in done:
        mark[...] = jnp.zeros_like(mark)
    mine, core, _ = place(g)
    seq = 1 - core if last_part else core
    forward, _ = halves_of(dims, windows, half)
    for piece, d in zip(pieces, partners(g)):
        come = lax.bitwise_xor(mine, d)
        for k in range(tiles):
            lanes = pl.ds(pl.multiple_of((come * tiles + k) * LANES, LANES), LANES)
            now[:, lanes] = piece[k * rows : (k + 1) * rows, :].astype(BF16)

    def send(whole):
        part = now.shape[1] // 4
        copies = []
        for k in range(4):
            lanes = pl.ds(k * part, part)
            copies.append(pltpu.make_async_copy(now.at[:, lanes], whole.at[seq, :, lanes], sent.at[k]))
        for copy in copies:
            copy.start()
        for copy in copies:
            copy.wait()

    if isinstance(forward, bool):
        send(mixed if forward else grad_v)
    else:
        pl.when(forward)(lambda: send(mixed))
        pl.when(jnp.logical_not(forward))(lambda: send(grad_v))


def shards(values, keys_b, queries_c, forget, skip, cotangent):
    seqs, rows, wide = values.shape
    head_count = skip.shape[0]
    state_size = keys_b.shape[-1]
    blocks = lax.axis_size("seq")
    peers = lax.axis_size("head")
    g = max(1, min(4, wide // LANES, blocks))
    windows = blocks // g
    heads = head_count // g
    tiles = wide // g // LANES
    dims = (g, rows, tiles, heads)
    window = g * rows
    width = tiles * LANES
    index = lax.axis_index("seq")
    vmem = pl.BlockSpec(memory_space=pltpu.VMEM)

    def swap(send, pieces):
        return [send(piece, d) for d, piece in zip(partners(g), pieces)]

    def same(piece, d):
        if d == 0:
            return piece
        return lax.ppermute(piece, "seq", [(i, i ^ d) for i in range(blocks)])

    def cross(piece, d):
        perm = [
            (i * peers + c, (i ^ d) * peers + (c ^ 1)) for i in range(blocks) for c in range(peers)
        ]
        return lax.ppermute(piece, ("seq", "head"), perm)

    def shape(*dims, dtype=F32):
        return jax.ShapeDtypeStruct(dims, dtype)

    hbm = pl.BlockSpec(memory_space=pltpu.HBM)

    def call(kernel, out, ins, scratch=(), after=(), far=(), far_out=(), aliases={}, limit=48):
        count, extra = len(ins), len(after)

        def body(*refs):
            kernel(*refs[:count], *refs[count + extra :])

        outs = pl.pallas_call(
            body,
            out_shape=out,
            in_specs=[hbm if n in far else vmem for n in range(count)] + [hbm] * extra,
            out_specs=[hbm if n in far_out else vmem for n in range(len(out))],
            scratch_shapes=list(scratch),
            input_output_aliases=aliases,
            cost_estimate=pl.CostEstimate(
                flops=0,
                bytes_accessed=sum(a.size * a.dtype.itemsize for a in list(ins) + list(out)),
                transcendentals=0,
            ),
            compiler_params=pltpu.CompilerParams(vmem_limit_bytes=limit * MIB),
        )(*ins, *after)
        return list(outs)

    base = 2 * tiles * rows
    got = []
    for shared in (True, False):
        pieces = call(
            functools.partial(pack_kernel, dims, shared),
            [shape(base + EXTRA + (2 * rows if shared else 0), LANES)] * g,
            [values, cotangent, keys_b, queries_c, forget, skip[None, :]],
            [
                pltpu.VMEM((rows, wide), BF16),
                pltpu.VMEM((rows, wide), BF16),
                pltpu.VMEM((rows, state_size), BF16),
                pltpu.VMEM((rows, state_size), BF16),
                pltpu.VMEM((head_count, rows), F32),
                pltpu.VMEM((1, head_count), F32),
                pltpu.SemaphoreType.DMA((8,)),
            ],
            far=range(6),
            limit=62 if shared else 48,
        )
        got.append(swap(same if shared else cross, pieces))
    rise = [(i, i + g) for i in range(blocks - g)]
    fall = [(i + g, i) for i in range(blocks - g)]
    map_shapes = [shape(window, state_size, dtype=BF16)] * 2
    own_shapes = [
        shape(window, width, dtype=BF16),
        shape(window, width, dtype=BF16),
        shape(EXTRA, window),
        shape(8, width),
    ]
    state_shape = shape(state_size, width)
    near = [(i, i ^ g) for i in range(blocks)]
    middle = [(i, i ^ (3 * g) if i // g in (1, 2) else i) for i in range(blocks)]
    outer = [(i, i ^ (2 * g)) for i in range(blocks) if i // g in (1, 2)]
    maps, sums, back = [], {}, {}
    own, weighted, ends, state, results = ({} for _ in range(5))

    def gather(n, after=()):
        outs = call(
            functools.partial(gather_kernel, dims, n == 0),
            own_shapes
            + (map_shapes if n == 0 else [])
            + [shape(window, width, dtype=BF16), shape(state_size + EXTRA, width)],
            got[n] + maps,
            [pltpu.VMEM((g, EXTRA, LANES), F32)],
            after=after,
        )
        own[n], outs = outs[:4], outs[4:]
        if n == 0:
            maps.extend(outs[:2])
            outs = outs[2:]
        weighted[n], ends[n] = outs[:1], outs[1:]

    def second(n, after=()):
        outs = call(
            functools.partial(second_kernel, dims),
            [shape(window, width, dtype=BF16), state_shape],
            own[n][:3] + maps,
            after=after,
        )
        weighted[n] += outs[:1]
        ends[n] += outs[1:]

    def local(n, after=()):
        results[n] = call(
            functools.partial(local_kernel, dims),
            [shape(window, width)] * 2 + [shape(window, state_size)] * 2,
            own[n] + maps,
            after=after,
        )

    def meet(n):
        state[n] = [lax.ppermute(ends[n][0], "seq", near)]

    def cross_pairs(n, after=()):
        pair = call(step_kernel, [state_shape], ends[n] + state[n], after=after)
        state[n] += [lax.ppermute(pair[0], "seq", perm) for perm in (middle, outer)]
        return pair

    def step(n, k, after=()):
        first, other = ends[n]
        if k == 1:
            moved = call(step_kernel, [state_shape], [first, other, state[n][-1]], after=after)
        else:
            moved = call(last_kernel, [state_shape], [first, state[n][-1]], after=after)
        state[n].append(lax.ppermute(moved[0], "seq", middle if k == 1 else near))
        return moved

    def chain(n):
        first, other = ends[n]
        first, decay = first[:state_size], first[state_size : state_size + 1]
        odd = lax.rem(lax.div(index, g), 2) == 1
        total = [jnp.where(odd, other, first), jnp.where(odd, first, other)]
        state[n] = [jnp.zeros_like(first)] * 2
        for k in range(windows - 1):
            moved = [decay * a + b for a, b in zip(state[n], total)]
            state[n] = [lax.ppermute(moved[0], "seq", rise), lax.ppermute(moved[1], "seq", fall)]

    def finish(n, half, after=()):
        if windows == 4:
            states = state[n][:1] if half == 0 else state[n]
        else:
            states = state[n][half : half + 1]
        outs = call(
            functools.partial(half_kernel, dims, windows, half, n == 1, n == 1),
            [shape((tiles + n) * rows, LANES)] * g + [shape(window, state_size)],
            [own[n][2]] + results[n] + (sums[half] if n else []) + maps + weighted[n] + states,
            [pltpu.VMEM((window, width), F32)],
            after=after,
        )
        sums[half] = outs[g:]
        back[n, half] = swap(cross if n else same, outs[:g])

    gather(0)
    if windows == 4:
        meet(0)
        second(0)
        local(0)
        gather(1, after=results[0][:1])
        meet(1)
        second(1)
        moved = step(0, 1, after=ends[1][:1])
        finish(0, 0, after=moved)
        local(1)
        cross_pairs(1, after=back[0, 0][1:3] + state[0][1:] + results[1][:1])
        finish(1, 0)
        step(0, 2)
        finish(0, 1, after=back[1, 0][1:2])
        finish(1, 1, after=back[1, 0][2:] + back[0, 1][1:3])
    else:
        gather(1)
        for n in range(2):
            second(n)
            chain(n)
            local(n)
            finish(n, 0)
            finish(n, 1)
    part = rows // peers
    outs, slices, done = [], [], []
    for n, half in ((0, 0), (0, 1), (1, 0), (1, 1)):
        marked = (n, half) != (1, 1)
        if n:
            shares = call(
                functools.partial(sum_kernel, dims),
                [shape(part, state_size)] * peers,
                back[n, half],
                [pltpu.VMEM((rows, state_size), F32)],
                after=done + sums[half],
            )
        outs = call(
            functools.partial(unpack_kernel, dims, windows, half, n == 1, marked),
            [shape(seqs, rows, wide, dtype=BF16)] * 2 + [shape(8, LANES)] * marked,
            back[n, half] + outs,
            [pltpu.VMEM((rows, wide), BF16), pltpu.SemaphoreType.DMA((4,))],
            far=(g, g + 1),
            far_out=(0, 1),
            aliases={g: 0, g + 1: 1} if outs else {},
        )
        outs, done = outs[:2], outs[2:]
        if n:
            come = [lax.ppermute(shares[e], "head", [(c, c ^ e) for c in range(peers)]) for e in range(1, peers)]
            ours = functools.reduce(jnp.add, come[1::2], shares[0])
            theirs = functools.reduce(jnp.add, come[2::2], come[0])
            even = lax.rem(lax.axis_index("head"), 2) == 0
            slices.append((jnp.where(even, theirs, ours), jnp.where(even, ours, theirs)))
    mixed, grad_v = outs
    low = lax.div(index, g) < 2 if windows == 4 else True
    grad_bc = jnp.stack(
        [jnp.stack([pick(low, a, b) for a, b in zip(*order)]) for order in (slices[::-1], slices)]
    )
    return mixed, grad_v, grad_bc


def solution(mesh):
    in_specs = (
        P(None, "seq", "head"),
        P(None, "seq", None),
        P(None, "seq", None),
        P(None, "head", "seq"),
        P("head"),
        P(None, "seq", "head"),
    )
    out_specs = (
        P(None, "seq", "head"),
        P(None, "seq", "head"),
        P(None, None, ("seq", "head"), None),
    )
    return jax.shard_map(shards, mesh=mesh, in_specs=in_specs, out_specs=out_specs, check_vma=False)
```

```python
import functools

import jax
import jax.numpy as jnp
from jax import lax
from jax.experimental import pallas as pl
from jax.experimental.pallas import tpu as pltpu
from jax.sharding import PartitionSpec as P

F32, BF16 = jnp.float32, jnp.bfloat16
LANES = 128
EXTRA = 8
MIB = 1024 * 1024


def nn(a, b):
    return lax.dot_general(a, b, (((1,), (0,)), ((), ())), preferred_element_type=F32)


def nt(a, b):
    return lax.dot_general(a, b, (((1,), (1,)), ((), ())), preferred_element_type=F32)


def tn(a, b):
    return lax.dot_general(a, b, (((0,), (0,)), ((), ())), preferred_element_type=F32)


def rows_of(block, rows):
    return pl.ds(pl.multiple_of(block * rows, rows), rows)


def partners(g):
    return [0, 2, 1, 3] if g == 4 else list(range(g))


def place(g):
    index = lax.axis_index("seq")
    return lax.rem(index, g), lax.rem(lax.axis_index("head"), 2), lax.div(index, g)


def pick(flag, one, zero):
    if isinstance(flag, bool):
        return one if flag else zero
    return jnp.where(flag, one, zero)


def spread(columns, heads, tiles):
    per = heads // tiles
    width = LANES // per
    lane = lax.broadcasted_iota(jnp.int32, (columns.shape[0], LANES), 1)
    out = []
    for k in range(tiles):
        wide = jnp.broadcast_to(columns[:, k * per : k * per + 1], lane.shape)
        for e in range(1, per):
            h = k * per + e
            wide = jnp.where(lane >= e * width, columns[:, h : h + 1], wide)
        out.append(wide)
    return jnp.concatenate(out, axis=1) if tiles > 1 else out[0]


def pack_kernel(dims, shared, values, cotangent, keys, queries, forget, skip, *refs):
    g, rows, tiles, heads = dims
    pieces, (v_now, dy_now, b_now, c_now, f_now, s_now, arrived) = refs[:g], refs[g:]
    mine, core, _ = place(g)
    seq = core if shared else 1 - core
    half = values.shape[2] // 2
    moves = [(forget.at[seq], f_now), (skip, s_now)]
    if shared:
        moves += [(keys.at[seq], b_now), (queries.at[seq], c_now)]
    for whole, now in ((values, v_now), (cotangent, dy_now)):
        for k in range(2):
            lanes = pl.ds(k * half, half)
            moves.append((whole.at[seq, :, lanes], now.at[:, lanes]))
    copies = [pltpu.make_async_copy(a, b, arrived.at[n]) for n, (a, b) in enumerate(moves)]
    for copy in copies:
        copy.start()
    upto = lax.broadcasted_iota(jnp.int32, (rows, rows), 0) <= lax.broadcasted_iota(
        jnp.int32, (rows, rows), 1
    )
    for copy in copies[:-4]:
        copy.wait()
    count = skip.shape[1]
    own = lax.broadcasted_iota(jnp.int32, (count, count), 0) == lax.broadcasted_iota(
        jnp.int32, (count, count), 1
    )
    skips = jnp.sum(jnp.where(own, s_now[...], 0.0), axis=1, keepdims=True)
    logcum = -lax.dot_general(
        f_now[...],
        upto.astype(F32),
        (((1,), (0,)), ((), ())),
        precision=lax.Precision.HIGHEST,
        preferred_element_type=F32,
    )
    held = jnp.concatenate([logcum, jnp.broadcast_to(skips, logcum.shape)], axis=1)
    for piece, d in zip(pieces, partners(g)):
        to = lax.bitwise_xor(mine, d)
        part = held[:heads]
        for j in range(1, g):
            part = jnp.where(to == j, held[j * heads : (j + 1) * heads], part)
        end = 2 * tiles * rows
        piece[end : end + heads, :] = part
        if heads < EXTRA:
            piece[end + heads : end + EXTRA, :] = jnp.zeros((EXTRA - heads, LANES), F32)
        if shared:
            piece[end + EXTRA : end + EXTRA + rows, :] = b_now[...].astype(F32)
            piece[end + EXTRA + rows : end + EXTRA + 2 * rows, :] = c_now[...].astype(F32)
    for w, now in enumerate((v_now, dy_now)):
        for copy in copies[len(copies) - 4 + 2 * w :][:2]:
            copy.wait()
        for piece, d in zip(pieces, partners(g)):
            to = lax.bitwise_xor(mine, d)
            for k in range(tiles):
                lanes = pl.ds(pl.multiple_of((to * tiles + k) * LANES, LANES), LANES)
                at = (w * tiles + k) * rows
                piece[at : at + rows, :] = now[:, lanes].astype(F32)


def gather_kernel(dims, shared, *refs):
    g, rows, tiles, heads = dims
    pieces, refs = refs[:g], refs[g:]
    if shared:
        v_all, dy_all, log_rows, skip_row, keys, queries = refs[:6]
    else:
        keys, queries, v_all, dy_all, log_rows, skip_row = refs[:6]
    weighted, first, blocks = refs[6:]
    window = g * rows
    mine, _, at_window = place(g)
    end = 2 * tiles * rows
    for piece, d in zip(pieces, partners(g)):
        at = lax.bitwise_xor(mine, d)
        here = rows_of(at, rows)
        for k in range(tiles):
            lanes = slice(k * LANES, (k + 1) * LANES)
            v_all[here, lanes] = piece[k * rows : (k + 1) * rows, :].astype(BF16)
            dy_all[here, lanes] = piece[(tiles + k) * rows : (tiles + k + 1) * rows, :].astype(BF16)
        blocks[at] = piece[end : end + EXTRA, :]
        if shared:
            keys[here, :] = piece[end + EXTRA : end + EXTRA + rows, :].astype(BF16)
            queries[here, :] = piece[end + EXTRA + rows : end + EXTRA + 2 * rows, :].astype(BF16)
    before = jnp.zeros((EXTRA, 1), F32)
    parts = []
    for j in range(g):
        block = blocks[j][:, :rows] + before
        before = block[:, rows - 1 : rows]
        parts.append(block)
    logs = jnp.concatenate(parts, axis=1)
    log_rows[...] = logs
    cols = jnp.transpose(logs)[:, :heads]
    skips = jnp.transpose(blocks[0])[rows : rows + 1, :heads]
    skip_row[...] = jnp.broadcast_to(spread(skips, heads, tiles), skip_row.shape)
    last = cols[window - 1 : window, :]
    odd = lax.rem(at_window, 2) == 1
    gain = spread(jnp.exp(jnp.where(odd, cols, last - cols)), heads, tiles)
    weighted[...] = (jnp.where(odd, dy_all[...], v_all[...]).astype(F32) * gain).astype(BF16)
    states = first.shape[0] - EXTRA
    first[:states, :] = tn(jnp.where(odd, queries[...], keys[...]), weighted[...])
    first[states:, :] = jnp.broadcast_to(spread(jnp.exp(last), heads, tiles), (EXTRA, tiles * LANES))


def second_kernel(dims, v_all, dy_all, log_rows, keys, queries, weighted, second):
    g, rows, tiles, heads = dims
    _, _, at_window = place(g)
    odd = lax.rem(at_window, 2) == 1
    cols = jnp.transpose(log_rows[...])[:, :heads]
    last = cols[g * rows - 1 :, :]
    gain = spread(jnp.exp(jnp.where(odd, last - cols, cols)), heads, tiles)
    weighted[...] = (jnp.where(odd, v_all[...], dy_all[...]).astype(F32) * gain).astype(BF16)
    second[...] = tn(jnp.where(odd, keys[...], queries[...]), weighted[...])


def local_kernel(dims, v_all, dy_all, log_rows, skip_row, keys, queries, mixed, grad_v, grad_b, grad_c):
    g, rows, tiles, heads = dims
    window = g * rows
    head_width = tiles * LANES // heads
    log_cols = jnp.transpose(log_rows[...])[:, :heads]
    skips = skip_row[:1, :]
    mixed[...] = v_all[...].astype(F32) * skips
    dy_t = jnp.transpose(dy_all[...])
    tile = min(window, 256)
    causal = lax.broadcasted_iota(jnp.int32, (tile, tile), 0) >= lax.broadcasted_iota(
        jnp.int32, (tile, tile), 1
    )
    count = window // tile
    dv_t = [[None] * count for _ in range(heads)]
    for q in range(count):
        t = slice(q * tile, (q + 1) * tile)
        for r in range(q + 1):
            u = slice(r * tile, (r + 1) * tile)
            scores = nt(queries[t, :], keys[u, :])
            score_grad = jnp.zeros((tile, tile), F32)
            for h in range(heads):
                lanes = slice(h * head_width, (h + 1) * head_width)
                gap = log_cols[t, h : h + 1] - log_rows[h : h + 1, u]
                if q == r:
                    mask = jnp.where(causal, jnp.exp(jnp.where(causal, gap, 0.0)), 0.0)
                else:
                    mask = jnp.exp(gap)
                weights = (scores * mask).astype(BF16)
                mixed[t, lanes] += nn(weights, v_all[u, lanes])
                grown = nn(dy_t[lanes, t], weights)
                dv_t[h][r] = grown if dv_t[h][r] is None else dv_t[h][r] + grown
                score_grad = score_grad + nt(dy_all[t, lanes], v_all[u, lanes]) * mask
            score_grad = score_grad.astype(BF16)
            c_part = nn(score_grad, keys[u, :])
            b_part = tn(score_grad, queries[t, :])
            if r == 0:
                grad_c[t, :] = c_part
            else:
                grad_c[t, :] += c_part
            if q == r:
                grad_b[u, :] = b_part
            else:
                grad_b[u, :] += b_part
    whole_t = jnp.concatenate([jnp.concatenate(parts, axis=1) for parts in dv_t], axis=0)
    grad_v[...] = jnp.transpose(whole_t) + dy_all[...].astype(F32) * skips


def step_kernel(first, second, near, pair):
    states = pair.shape[0]
    pair[...] = first[states : states + 1, :] * near[:states, :] + second[...]


def last_kernel(first, far, moved):
    states = moved.shape[0]
    moved[...] = first[states : states + 1, :] * far[...] + first[:states, :]


def halves_of(dims, windows, half):
    _, _, at = place(dims[0])
    if windows != 4:
        return half == 0, None
    low = at < 2
    return (low if half == 0 else at >= 2), (at == 1) | (at == 2)


def half_kernel(dims, windows, half, last_part, doubled, log_rows, mixed, grad_v, grad_b, grad_c, *refs):
    g, rows, tiles, heads = dims
    if last_part:
        other, refs = refs[0], refs[1:]
    keys, queries, to_first, to_second, refs = *refs[:4], refs[4:]
    states, refs = refs[: len(refs) - g - 2], refs[len(refs) - g - 2 :]
    pieces, total, whole = refs[:g], refs[g], refs[g + 1]
    window = g * rows
    mine, _, at_window = place(g)
    forward, inner = halves_of(dims, windows, half)
    if inner is None:
        state = states[0][...]
    else:
        count = keys.shape[1]
        near = states[0][:count, :]
        if half == 0:
            state = jnp.where(inner, near, 0.0)
        else:
            outer = states[2][...]
            if doubled:
                outer = states[0][count : count + 1, :] * outer + near
            state = jnp.where(inner, states[1][...], outer)
    state = state.astype(BF16)
    cols = jnp.transpose(log_rows[...])[:, :heads]
    last = cols[window - 1 : window, :]
    gain = spread(jnp.exp(pick(forward, cols, last - cols)), heads, tiles)
    more = gain * nn(pick(forward, queries[...], keys[...]), state)
    whole[...] = pick(forward, mixed[...], grad_v[...]) + more
    odd = lax.rem(at_window, 2) == 1
    used = odd if forward is True else jnp.logical_not(odd) if forward is False else odd == forward
    summed = pick(forward, grad_c[...], grad_b[...]) + nt(jnp.where(used, to_first[...], to_second[...]), state)
    if last_part:
        summed = summed + other[...]
    total[...] = summed
    for piece, d in zip(pieces, partners(g)):
        here = rows_of(lax.bitwise_xor(mine, d), rows)
        for k in range(tiles):
            piece[k * rows : (k + 1) * rows, :] = whole[here, k * LANES : (k + 1) * LANES]
        if last_part:
            piece[tiles * rows : (tiles + 1) * rows, :] = total[here, :]


def sum_kernel(dims, *refs):
    g, rows, tiles, heads = dims
    pieces, shares, total = refs[:g], refs[g:-1], refs[-1]
    at = slice(tiles * rows, (tiles + 1) * rows)
    total[...] = functools.reduce(jnp.add, [piece[at, :] for piece in pieces])
    for e, share in enumerate(shares):
        part = rows // len(shares)
        share[...] = total[rows_of(lax.bitwise_xor(lax.axis_index("head"), e), part), :]


def unpack_kernel(dims, windows, half, last_part, marked, *refs):
    g, rows, tiles, heads = dims
    pieces, refs = refs[:g], refs[g:]
    mixed, grad_v, *done, now, sent = refs[-5:] if marked else refs[-4:]
    for mark in done:
        mark[...] = jnp.zeros_like(mark)
    mine, core, _ = place(g)
    seq = 1 - core if last_part else core
    forward, _ = halves_of(dims, windows, half)
    width = tiles * LANES

    def send(whole):
        copies = []
        for n, (piece, d) in enumerate(zip(pieces, partners(g))):
            come = lax.bitwise_xor(mine, d)
            for k in range(tiles):
                lanes = pl.ds(pl.multiple_of(come * width + k * LANES, LANES), LANES)
                now[:, lanes] = piece[k * rows : (k + 1) * rows, :].astype(BF16)
            lanes = pl.ds(pl.multiple_of(come * width, width), width)
            copies.append(pltpu.make_async_copy(now.at[:, lanes], whole.at[seq, :, lanes], sent.at[n]))
            copies[-1].start()
        for copy in copies:
            copy.wait()

    if isinstance(forward, bool):
        send(mixed if forward else grad_v)
    else:
        pl.when(forward)(lambda: send(mixed))
        pl.when(jnp.logical_not(forward))(lambda: send(grad_v))


def shards(values, keys_b, queries_c, forget, skip, cotangent):
    seqs, rows, wide = values.shape
    head_count = skip.shape[0]
    state_size = keys_b.shape[-1]
    blocks = lax.axis_size("seq")
    peers = lax.axis_size("head")
    g = max(1, min(4, wide // LANES, blocks))
    windows = blocks // g
    heads = head_count // g
    tiles = wide // g // LANES
    dims = (g, rows, tiles, heads)
    window = g * rows
    width = tiles * LANES
    index = lax.axis_index("seq")
    vmem = pl.BlockSpec(memory_space=pltpu.VMEM)

    def swap(send, pieces):
        return [send(piece, d) for d, piece in zip(partners(g), pieces)]

    def same(piece, d):
        if d == 0:
            return piece
        return lax.ppermute(piece, "seq", [(i, i ^ d) for i in range(blocks)])

    def cross(piece, d):
        perm = [
            (i * peers + c, (i ^ d) * peers + (c ^ 1)) for i in range(blocks) for c in range(peers)
        ]
        return lax.ppermute(piece, ("seq", "head"), perm)

    def shape(*dims, dtype=F32):
        return jax.ShapeDtypeStruct(dims, dtype)

    hbm = pl.BlockSpec(memory_space=pltpu.HBM)

    def call(kernel, out, ins, scratch=(), after=(), far=(), far_out=(), aliases={}, limit=48):
        count, extra = len(ins), len(after)

        def body(*refs):
            kernel(*refs[:count], *refs[count + extra :])

        outs = pl.pallas_call(
            body,
            out_shape=out,
            in_specs=[hbm if n in far else vmem for n in range(count)] + [hbm] * extra,
            out_specs=[hbm if n in far_out else vmem for n in range(len(out))],
            scratch_shapes=list(scratch),
            input_output_aliases=aliases,
            cost_estimate=pl.CostEstimate(
                flops=0,
                bytes_accessed=sum(a.size * a.dtype.itemsize for a in list(ins) + list(out)),
                transcendentals=0,
            ),
            compiler_params=pltpu.CompilerParams(vmem_limit_bytes=limit * MIB),
        )(*ins, *after)
        return list(outs)

    base = 2 * tiles * rows
    got = []
    for shared in (True, False):
        pieces = call(
            functools.partial(pack_kernel, dims, shared),
            [shape(base + EXTRA + (2 * rows if shared else 0), LANES)] * g,
            [values, cotangent, keys_b, queries_c, forget, skip[None, :]],
            [
                pltpu.VMEM((rows, wide), BF16),
                pltpu.VMEM((rows, wide), BF16),
                pltpu.VMEM((rows, state_size), BF16),
                pltpu.VMEM((rows, state_size), BF16),
                pltpu.VMEM((head_count, rows), F32),
                pltpu.VMEM((1, head_count), F32),
                pltpu.SemaphoreType.DMA((8,)),
            ],
            far=range(6),
            limit=62 if shared else 48,
        )
        got.append(swap(same if shared else cross, pieces))
    rise = [(i, i + g) for i in range(blocks - g)]
    fall = [(i + g, i) for i in range(blocks - g)]
    map_shapes = [shape(window, state_size, dtype=BF16)] * 2
    own_shapes = [
        shape(window, width, dtype=BF16),
        shape(window, width, dtype=BF16),
        shape(EXTRA, window),
        shape(8, width),
    ]
    state_shape = shape(state_size, width)
    near = [(i, i ^ g) for i in range(blocks)]
    middle = [(i, i ^ (3 * g) if i // g in (1, 2) else i) for i in range(blocks)]
    outer = [(i, i ^ (2 * g)) for i in range(blocks) if i // g in (1, 2)]
    maps, sums, back = [], {}, {}
    own, weighted, ends, state, results = ({} for _ in range(5))

    def gather(n, after=()):
        outs = call(
            functools.partial(gather_kernel, dims, n == 0),
            own_shapes
            + (map_shapes if n == 0 else [])
            + [shape(window, width, dtype=BF16), shape(state_size + EXTRA, width)],
            got[n] + maps,
            [pltpu.VMEM((g, EXTRA, LANES), F32)],
            after=after,
        )
        own[n], outs = outs[:4], outs[4:]
        if n == 0:
            maps.extend(outs[:2])
            outs = outs[2:]
        weighted[n], ends[n] = outs[:1], outs[1:]

    def second(n, after=()):
        outs = call(
            functools.partial(second_kernel, dims),
            [shape(window, width, dtype=BF16), state_shape],
            own[n][:3] + maps,
            after=after,
        )
        weighted[n] += outs[:1]
        ends[n] += outs[1:]

    def local(n, after=()):
        results[n] = call(
            functools.partial(local_kernel, dims),
            [shape(window, width)] * 2 + [shape(window, state_size)] * 2,
            own[n] + maps,
            after=after,
        )

    def meet(n):
        state[n] = [lax.ppermute(ends[n][0], "seq", near)]

    def cross_pairs(n, after=()):
        pair = call(step_kernel, [state_shape], ends[n] + state[n], after=after)
        state[n] += [lax.ppermute(pair[0], "seq", perm) for perm in (middle, outer)]
        return pair

    def step(n, k, after=()):
        first, other = ends[n]
        if k == 1:
            moved = call(step_kernel, [state_shape], [first, other, state[n][-1]], after=after)
        else:
            moved = call(last_kernel, [state_shape], [first, state[n][-1]], after=after)
        state[n].append(lax.ppermute(moved[0], "seq", middle if k == 1 else near))
        return moved

    def chain(n):
        first, other = ends[n]
        first, decay = first[:state_size], first[state_size : state_size + 1]
        odd = lax.rem(lax.div(index, g), 2) == 1
        total = [jnp.where(odd, other, first), jnp.where(odd, first, other)]
        state[n] = [jnp.zeros_like(first)] * 2
        for k in range(windows - 1):
            moved = [decay * a + b for a, b in zip(state[n], total)]
            state[n] = [lax.ppermute(moved[0], "seq", rise), lax.ppermute(moved[1], "seq", fall)]

    def finish(n, half, after=()):
        if windows == 4:
            states = state[n][:1] if half == 0 else state[n]
        else:
            states = state[n][half : half + 1]
        outs = call(
            functools.partial(half_kernel, dims, windows, half, n == 1, n == 1),
            [shape((tiles + n) * rows, LANES)] * g + [shape(window, state_size)],
            [own[n][2]] + results[n] + (sums[half] if n else []) + maps + weighted[n] + states,
            [pltpu.VMEM((window, width), F32)],
            after=after,
        )
        sums[half] = outs[g:]
        back[n, half] = swap(cross if n else same, outs[:g])

    gather(0)
    if windows == 4:
        meet(0)
        second(0)
        local(0)
        gather(1, after=results[0][:1])
        meet(1)
        second(1)
        moved = step(0, 1, after=ends[1][:1])
        finish(0, 0, after=moved)
        local(1)
        cross_pairs(1, after=back[0, 0][1:3] + state[0][1:] + results[1][:1])
        finish(1, 0)
        step(0, 2)
        finish(0, 1, after=back[1, 0][1:2])
        finish(1, 1, after=back[1, 0][2:] + back[0, 1][1:3])
    else:
        gather(1)
        for n in range(2):
            second(n)
            chain(n)
            local(n)
            finish(n, 0)
            finish(n, 1)
    part = rows // peers
    outs, slices, done = [], [], []
    for n, half in ((0, 0), (0, 1), (1, 0), (1, 1)):
        marked = (n, half) != (1, 1)
        if n:
            shares = call(
                functools.partial(sum_kernel, dims),
                [shape(part, state_size)] * peers,
                back[n, half],
                [pltpu.VMEM((rows, state_size), F32)],
                after=done + sums[half],
            )
        outs = call(
            functools.partial(unpack_kernel, dims, windows, half, n == 1, marked),
            [shape(seqs, rows, wide, dtype=BF16)] * 2 + [shape(8, LANES)] * marked,
            back[n, half] + outs,
            [pltpu.VMEM((rows, wide), BF16), pltpu.SemaphoreType.DMA((g,))],
            far=(g, g + 1),
            far_out=(0, 1),
            aliases={g: 0, g + 1: 1} if outs else {},
        )
        outs, done = outs[:2], outs[2:]
        if n:
            come = [lax.ppermute(shares[e], "head", [(c, c ^ e) for c in range(peers)]) for e in range(1, peers)]
            ours = functools.reduce(jnp.add, come[1::2], shares[0])
            theirs = functools.reduce(jnp.add, come[2::2], come[0])
            even = lax.rem(lax.axis_index("head"), 2) == 0
            slices.append((jnp.where(even, theirs, ours), jnp.where(even, ours, theirs)))
    mixed, grad_v = outs
    low = lax.div(index, g) < 2 if windows == 4 else True
    grad_bc = jnp.stack(
        [jnp.stack([pick(low, a, b) for a, b in zip(*order)]) for order in (slices[::-1], slices)]
    )
    return mixed, grad_v, grad_bc


def solution(mesh):
    in_specs = (
        P(None, "seq", "head"),
        P(None, "seq", None),
        P(None, "seq", None),
        P(None, "head", "seq"),
        P("head"),
        P(None, "seq", "head"),
    )
    out_specs = (
        P(None, "seq", "head"),
        P(None, "seq", "head"),
        P(None, None, ("seq", "head"), None),
    )
    return jax.shard_map(shards, mesh=mesh, in_specs=in_specs, out_specs=out_specs, check_vma=False)
```
